32 devices in a mesh: col: 4 (over y, x), row: 8 (over z, core).
Axes of the slice: x: 2, y: 2, z: 4, core: 2. Of those that a mesh axis runs over, the one named last changes fastest.
Arguments:
- true_ids: int32 [65536], P(('col', 'row')), may hold values from 4 to 28
- picked: int32 [65536], P(('col', 'row')), may hold values from 0 to 1, as said below
- replace_kinds: int32 [65536], P(('col', 'row')), may hold values from 0 to 9
- random_ids: int32 [65536], P(('col', 'row')), may hold values from 4 to 28
- splits: int32 [64], P(('col', 'row')), may hold values from 0 to 1, as said below
- embedding: float32 [33, 640], replicated, may hold values from -0.6 to 0.6
- projection: float32 [640, 1920], replicated, may hold values from -0.25 to 0.25
- outward: float32 [640, 640], replicated, may hold values from -1 to 1
- feedforward: float32 [2, 640, 2560], P(None, 'row', 'col'), may hold values from -0.25 to 0.25
- vectors: float32 [15, 640], replicated
- embedding_drift: float32 [33, 640], replicated, may hold values from -1.335144e-05 to 1.335144e-05
- embedding_spread: float32 [33, 640], replicated, may hold values from 8.0874744e-13 to 3.2349898e-12
- projection_drift: float32 [640, 1920], replicated, may hold values from -1.335144e-05 to 1.335144e-05
- projection_spread: float32 [640, 1920], replicated, may hold values from 8.0874744e-13 to 3.2349898e-12
- outward_drift: float32 [640, 640], replicated, may hold values from -1.335144e-05 to 1.335144e-05
- outward_spread: float32 [640, 640], replicated, may hold values from 8.0874744e-13 to 3.2349898e-12
- feedforward_drift: float32 [2, 640, 2560], P(None, 'row', 'col'), may hold values from -1.335144e-05 to 1.335144e-05
- feedforward_spread: float32 [2, 640, 2560], P(None, 'row', 'col'), may hold values from 8.0874744e-13 to 3.2349898e-12
- vectors_drift: float32 [15, 640], replicated, may hold values from -5.340576e-05 to 5.340576e-05
- vectors_spread: float32 [15, 640], replicated, may hold values from 1.2939959e-11 to 5.1759836e-11
Outputs:
- loss_pair: float32 [2], replicated
- grad_norm: float32 [], replicated
- embedding_next: float32 [33, 640], replicated
- embedding_moved: float32 [33, 640], replicated
- embedding_varied: float32 [33, 640], replicated
- embedding_copy: bfloat16 [33, 640], replicated
- projection_next: float32 [640, 1920], replicated
- projection_moved: float32 [640, 1920], replicated
- projection_varied: float32 [640, 1920], replicated
- projection_copy: bfloat16 [640, 1920], replicated
- outward_next: float32 [640, 640], replicated
- outward_moved: float32 [640, 640], replicated
- outward_varied: float32 [640, 640], replicated
- outward_copy: bfloat16 [640, 640], replicated
- feedforward_next: float32 [2, 640, 2560], P(None, 'row', 'col')
- feedforward_moved: float32 [2, 640, 2560], P(None, 'row', 'col')
- feedforward_varied: float32 [2, 640, 2560], P(None, 'row', 'col')
- feedforward_copy: bfloat16 [2, 640, 2560], P(None, 'row', 'col')
- vectors_next: float32 [15, 640], replicated
- vectors_moved: float32 [15, 640], replicated
- vectors_varied: float32 [15, 640], replicated
- vectors_copy: bfloat16 [15, 640], replicated
The draws below stay inside these ranges and needn't reach their ends.
Inputs may be any that keep to these rules, and one draw needn't show every extreme that they name: Each half of every slot of 1024 positions holds at least one picked position. `replace_kinds`: 0 to 7 mask a picked position, 8 replaces it by random_ids, 9 keeps it; unpicked positions keep true_ids. `splits`: the last slot is always split.
All inputs are finite; a program needn't handle non-finite values.
Results may differ from the reference program's by a relative error of at most 0.0088.
Values may be sent and summed in bfloat16 or wider, within the bound.
No kernel may reach another device: no remote copies, remote signals or barrier semaphores. Data moves between devices by JAX's collectives and lax.ppermute only.
A program may use at most 512 MiB of HBM per device.

```python
import math
import jax
import jax.numpy as jnp
from jax import lax

D = 640
HEADS = 20
HEAD_DIM = 32
FF = 2560
V = 33
SLOT = 1024
STEP = 10
TOKENS = 65536
SLOTS_ALL = 64


def draw_picked(key, part):
    key = jax.random.fold_in(key, 11)
    first_key, second_key = jax.random.split(key)
    base = jax.random.randint(first_key, (TOKENS,), 0, 20) < 3
    half_rows = SLOT // 2
    spots = jax.random.randint(second_key, (TOKENS // half_rows, 1), 0, half_rows)
    forced = (jnp.arange(half_rows, dtype=jnp.int32)[None, :] == spots).reshape(-1)
    return (base | forced).astype(jnp.int32)


def draw_splits(key, part):
    key = jax.random.fold_in(key, 12)
    index = jnp.arange(SLOTS_ALL, dtype=jnp.int32)
    level = jax.random.randint(key, (SLOTS_ALL,), 0, SLOTS_ALL)
    return (level <= index).astype(jnp.int32)


def draw_vectors(key, part):
    key = jax.random.fold_in(key, 13)
    first_key, second_key = jax.random.split(key)
    row_total = 11 + FF // D
    shifts = 0.2 * jax.random.normal(first_key, (row_total, D), jnp.float32)
    gains = 1.0 + 0.2 * jax.random.normal(second_key, (row_total, D), jnp.float32)
    index = jnp.arange(row_total, dtype=jnp.int32)
    is_gain = (index == 0) | (index == 6) | (index == 9 + FF // D)
    return jnp.where(is_gain[:, None], gains, shifts)


def with_ends(values, rng, smallest, high):
    extent = values.shape
    place = [jax.random.randint(jax.random.fold_in(rng, axis), (), 0, extent[axis]) for axis in range(len(extent))]
    values = values.at[tuple(place)].set(smallest)
    longest = extent.index(max(extent))
    place[longest] = (place[longest] + 1) % extent[longest]
    return values.at[tuple(place)].set(high)


def block_levels(rng, shape, pieces, least, high):
    def one(axis_at, parts):
        steps = jax.random.uniform(jax.random.fold_in(jax.random.fold_in(rng, 6), axis_at), (parts,), jnp.float32, least / len(pieces), high / len(pieces))
        return jnp.repeat(jnp.exp(steps), shape[axis_at] // parts).reshape((-1,) + (1,) * (len(shape) - axis_at - 1))

    gain = one(*pieces[0])
    for cut in pieces[1:]:
        gain = gain * one(*cut)
    return gain


def normal_values(key, dims, deviation, most, cuts=(), held_as=jnp.bfloat16):
    values = jax.random.normal(key, dims, jnp.float32) * deviation
    if len(cuts) > 0:
        values = block_levels(key, dims, cuts, -0.22, 0.18) * values
    return jnp.clip(values, min=-most, max=most).astype(held_as)


def setup_inputs(seed: int = 0) -> dict:
    keys = jax.random.split(jax.random.key(seed), 21)
    true_ids = with_ends(jax.random.randint(keys[0], (TOKENS,), 4, 29), jax.random.fold_in(keys[0], 1), 4, 28).astype(jnp.int32)
    picked = draw_picked(jax.random.fold_in(keys[20], 71), 0)
    replace_kinds = with_ends(jax.random.randint(keys[2], (TOKENS,), 0, 10), jax.random.fold_in(keys[2], 1), 0, 9).astype(jnp.int32)
    random_ids = with_ends(jax.random.randint(keys[3], (TOKENS,), 4, 29), jax.random.fold_in(keys[3], 1), 4, 28).astype(jnp.int32)
    splits = draw_splits(jax.random.fold_in(keys[20], 71), 0)
    embedding = normal_values(keys[5], (V, D), 0.1, 0.6, (), jnp.float32)
    projection = normal_values(keys[6], (D, 3 * D), D ** -0.5, 0.25, (), jnp.float32)
    outward = normal_values(keys[7], (D, D), (D // 16) ** -0.5, 1.0, (), jnp.float32)
    feedforward = normal_values(keys[8], (2, D, FF), D ** -0.5, 0.25, ((1, 8), (2, 4)), jnp.float32)
    vectors = draw_vectors(jax.random.fold_in(keys[20], 71), 0)
    embedding_drift = normal_values(keys[10], (V, D), (0.002 * (V * D + 4 * D * D + (11 + FF // D) * D + 2 * D * FF) ** -0.5), 1.33514404296875e-05, (), jnp.float32)
    embedding_spread = jnp.clip(jnp.exp(jax.random.uniform(keys[11], (V, D), jnp.float32, math.log(8.087474375091663e-13), math.log(3.2349897500366653e-12))), 8.087474375091663e-13, 3.2349897500366653e-12)
    projection_drift = normal_values(keys[12], (D, 3 * D), (0.002 * (V * D + 4 * D * D + (11 + FF // D) * D + 2 * D * FF) ** -0.5), 1.33514404296875e-05, (), jnp.float32)
    projection_spread = jnp.clip(jnp.exp(jax.random.uniform(keys[13], (D, 3 * D), jnp.float32, math.log(8.087474375091663e-13), math.log(3.2349897500366653e-12))), 8.087474375091663e-13, 3.2349897500366653e-12)
    outward_drift = normal_values(keys[14], (D, D), (0.002 * (V * D + 4 * D * D + (11 + FF // D) * D + 2 * D * FF) ** -0.5), 1.33514404296875e-05, (), jnp.float32)
    outward_spread = jnp.clip(jnp.exp(jax.random.uniform(keys[15], (D, D), jnp.float32, math.log(8.087474375091663e-13), math.log(3.2349897500366653e-12))), 8.087474375091663e-13, 3.2349897500366653e-12)
    feedforward_drift = normal_values(keys[16], (2, D, FF), (0.002 * (V * D + 4 * D * D + (11 + FF // D) * D + 2 * D * FF) ** -0.5), 1.33514404296875e-05, ((1, 8), (2, 4)), jnp.float32)
    feedforward_spread = jnp.clip(jnp.exp(math.log(3.2349897500366653e-12) - 1.3862944 * jax.random.uniform(keys[17], (2, D, FF), jnp.float32) ** block_levels(keys[17], (2, D, FF), ((1, 8), (2, 4)), -0.2, 0.2)), 8.087474375091663e-13, 3.2349897500366653e-12)
    vectors_drift = normal_values(keys[18], (11 + FF // D, D), (0.008 * (V * D + 4 * D * D + (11 + FF // D) * D + 2 * D * FF) ** -0.5), 5.340576171875e-05, (), jnp.float32)
    vectors_spread = jnp.clip(jnp.exp(jax.random.uniform(keys[19], (11 + FF // D, D), jnp.float32, math.log(1.2939959000146661e-11), math.log(5.1759836000586645e-11))), 1.2939959000146661e-11, 5.1759836000586645e-11)
    return dict(true_ids=true_ids, picked=picked, replace_kinds=replace_kinds, random_ids=random_ids, splits=splits, embedding=embedding, projection=projection, outward=outward, feedforward=feedforward, vectors=vectors, embedding_drift=embedding_drift, embedding_spread=embedding_spread, projection_drift=projection_drift, projection_spread=projection_spread, outward_drift=outward_drift, outward_spread=outward_spread, feedforward_drift=feedforward_drift, feedforward_spread=feedforward_spread, vectors_drift=vectors_drift, vectors_spread=vectors_spread)


@jax.custom_vjp
def low(v):
    return lax.optimization_barrier(v.astype(jnp.bfloat16)).astype(jnp.float32)

@jax.custom_vjp
def low_back(v):
    return v

def low_keep(v):
    return (low(v), None)

def low_pass(kept, grad):
    return (grad,)

def back_keep(v):
    return (v, None)

def back_low(kept, grad):
    return (low(grad),)
low.defvjp(low_keep, low_pass)
low_back.defvjp(back_keep, back_low)
PRECISE = lax.Precision.HIGHEST
EPS_NORM = 1e-05
CLIP_NORM = 0.002
FIRST_DECAY = 0.5
SECOND_DECAY = 0.5
ADAM_EPS = 1e-08
WEIGHT_DECAY = 0.01
MASK_ID = 32

def layer_norm(values, gain_row, shift_row):
    center = values - lax.optimization_barrier(jnp.mean(values, axis=-1, keepdims=True))
    spread = lax.optimization_barrier(jnp.mean(center * center, axis=-1, keepdims=True))
    return center * lax.rsqrt(spread + EPS_NORM) * gain_row + shift_row

def rotary(values, cos_table, sin_table):
    half_dim = values.shape[-1] // 2
    turned = jnp.concatenate([-values[..., half_dim:], values[..., :half_dim]], axis=-1)
    return values * cos_table[:, None, :] + turned * sin_table[:, None, :]

def rotary_tables(positions):
    freq = 10000.0 ** (-jnp.arange(0, HEAD_DIM, 2, dtype=jnp.float32) / HEAD_DIM)
    angle = positions.astype(jnp.float32)[:, None] * freq[None, :]
    angle = jnp.concatenate([angle, angle], axis=1)
    return (jnp.cos(angle), jnp.sin(angle))

def inputs_of(true_ids, picked, replace_kinds, random_ids):
    masked = (picked == 1) & (replace_kinds < 8)
    swapped = (picked == 1) & (replace_kinds == 8)
    return jnp.where(masked, MASK_ID, jnp.where(swapped, random_ids, true_ids)).astype(jnp.int32)

def adam_step(weight, grad, drift, spread, rate):
    drift = FIRST_DECAY * drift + (1.0 - FIRST_DECAY) * grad
    spread = SECOND_DECAY * spread + (1.0 - SECOND_DECAY) * grad * grad
    adjusted = drift / (1.0 - FIRST_DECAY ** STEP) / (jnp.sqrt(spread / (1.0 - SECOND_DECAY ** STEP)) + ADAM_EPS)
    return (weight - rate * (adjusted + WEIGHT_DECAY * weight), drift, spread)

def slot_loss(params, input_ids, targets, picked, split):
    embedding, projection, outward, feedforward, vectors = params
    slot_rows = input_ids.shape[0]
    bias_rows = FF // D
    within = jnp.arange(slot_rows, dtype=jnp.int32)
    second = (within >= slot_rows // 2).astype(jnp.int32) * split
    cos_table, sin_table = rotary_tables(within - second * (slot_rows // 2))
    embedded = embedding[input_ids]
    normed = low(layer_norm(embedded, vectors[0], vectors[1]))
    mixed = jnp.dot(normed, low(projection), precision=PRECISE) + vectors[2:5].reshape(-1)
    mixed = low_back(mixed)
    queries = low(rotary(mixed[:, :D].reshape(slot_rows, HEADS, HEAD_DIM), cos_table, sin_table))
    key_rows = low(rotary(mixed[:, D:2 * D].reshape(slot_rows, HEADS, HEAD_DIM), cos_table, sin_table))
    value_rows = low(mixed[:, 2 * D:].reshape(slot_rows, HEADS, HEAD_DIM))
    scores = jnp.einsum('qhe,khe->hqk', queries, key_rows, precision=PRECISE) * HEAD_DIM ** (-0.5)
    same = second[:, None] == second[None, :]
    scores = low_back(jnp.where(same[None], scores, -1e+30))
    probability = low(jax.nn.softmax(scores, axis=-1))
    attended = jnp.einsum('hqk,khe->qhe', probability, value_rows, precision=PRECISE).reshape(slot_rows, D)
    attended = low(low_back(attended))
    residual_one = embedded + low_back(jnp.dot(attended, low(outward), precision=PRECISE) + vectors[5])
    normed_two = low(layer_norm(residual_one, vectors[6], vectors[7]))
    wide = low(feedforward)
    hidden = low_back(jnp.dot(normed_two, wide[0], precision=PRECISE) + vectors[8:8 + bias_rows].reshape(-1))
    active = low(jax.nn.gelu(hidden, approximate=False))
    branch = jnp.dot(active, wide[1].T, precision=PRECISE) + vectors[8 + bias_rows]
    residual_two = residual_one + low_back(branch)
    final_out = low(layer_norm(residual_two, vectors[9 + bias_rows], vectors[10 + bias_rows]))
    logits = low_back(jnp.dot(final_out, low(embedding).T, precision=PRECISE))
    log_total = jax.nn.logsumexp(logits, axis=-1)
    chosen = jnp.take_along_axis(logits, targets[:, None], axis=1)[:, 0]
    pick_float = picked.astype(jnp.float32)
    second_float = second.astype(jnp.float32)
    first_count = jnp.sum(pick_float * (1.0 - second_float))
    second_count = jnp.sum(pick_float * second_float)
    crop_count = jnp.where(second == 1, second_count, first_count)
    return jnp.sum(pick_float * (log_total - chosen) / crop_count)

def reference(true_ids, picked, replace_kinds, random_ids, splits, embedding, projection, outward, feedforward, vectors, embedding_drift, embedding_spread, projection_drift, projection_spread, outward_drift, outward_spread, feedforward_drift, feedforward_spread, vectors_drift, vectors_spread):
    input_ids = inputs_of(true_ids, picked, replace_kinds, random_ids)
    slot_total = splits.shape[0]
    slot_rows = true_ids.shape[0] // slot_total
    crops = jnp.sum(1 + splits).astype(jnp.float32)

    def objective(params):

        def advance(carry, index):

            def piece(array):
                return lax.dynamic_slice_in_dim(array, index * slot_rows, slot_rows)
            value = jax.checkpoint(slot_loss)(params, piece(input_ids), piece(true_ids), piece(picked), splits[index])
            return (carry + value, None)
        summed, _ = lax.scan(advance, jnp.zeros((), jnp.float32), jnp.arange(slot_total, dtype=jnp.int32))
        return (summed / crops, summed)
    params = (embedding, projection, outward, feedforward, vectors)
    loss, backward, loss_sum = jax.vjp(objective, params, has_aux=True)
    grads = backward(jnp.ones((), jnp.float32))[0]
    squares = jnp.zeros((), jnp.float32)
    for grad in grads:
        squares = squares + jnp.sum(grad * grad)
    grad_norm = jnp.sqrt(squares)
    factor = jnp.minimum(1.0, CLIP_NORM / (grad_norm + 1e-06))
    drifts = (embedding_drift, projection_drift, outward_drift, feedforward_drift, vectors_drift)
    spreads = (embedding_spread, projection_spread, outward_spread, feedforward_spread, vectors_spread)
    step_rates = (0.05, 0.05, 0.1, 0.05, 0.2)
    results = [jnp.stack([loss_sum, crops]), grad_norm]
    for weight, grad, drift, spread, rate in zip(params, grads, drifts, spreads, step_rates):
        fresh, moved, varied = adam_step(weight, grad * factor, drift, spread, rate)
        results.extend([fresh, moved, varied, fresh.astype(jnp.bfloat16)])
    return tuple(results)
```

```python
import functools
import math

import jax
import jax.numpy as jnp
import numpy as np
from jax import lax
from jax.experimental import pallas as pl
from jax.experimental.pallas import tpu as pltpu
from jax.sharding import PartitionSpec as P

HEAD_DIM = 32
HALF = HEAD_DIM // 2
EXT = HEAD_DIM + 16
FF = 2560
STEP = 10
VPAD = 48
THIRD = 40
REST_TABLE = 32

EPS_NORM = 1e-05
CLIP_NORM = 0.002
FIRST_DECAY = 0.5
SECOND_DECAY = 0.5
ADAM_EPS = 1e-08
WEIGHT_DECAY = 0.01
MASK_ID = 32
MASKED = 1e30

LOG2E = math.log2(math.e)
SCALE = HEAD_DIM ** (-0.5)
MIB = 2**20

bf16 = jnp.bfloat16
f32 = jnp.float32

NN = ((1,), (0,))
NT = ((1,), (1,))
TN = ((0,), (0,))


def dot(left, right, dims=NN):
    return lax.dot_general(left, right, (dims, ((), ())), preferred_element_type=f32)


def split3(values):
    high = values.astype(bf16).astype(f32)
    rest = values - high
    middle = rest.astype(bf16).astype(f32)
    return high, middle, rest - middle


def norm_stats(values):
    center = values - jnp.mean(values, axis=0, keepdims=True)
    inverse = lax.rsqrt(jnp.mean(center * center, axis=0, keepdims=True) + EPS_NORM)
    return center * inverse, inverse


def norm_back(grad, hat, inverse, gain):
    scaled = grad * gain
    return inverse * (
        scaled
        - jnp.mean(scaled, axis=0, keepdims=True)
        - hat * jnp.mean(scaled * hat, axis=0, keepdims=True)
    )


def rows_of(count, width):
    return lax.broadcasted_iota(jnp.int32, (count, width), 0)


def lane_sum(values):
    return jnp.sum(values, axis=1, keepdims=True)


def columns_of(vectors, wide):
    wide[...] = jnp.zeros_like(wide)
    wide[0 : vectors.shape[0], :] = vectors[...]
    return wide[...].T


def qkv_kernel(
    meta, embedding, projection, vectors, cos_a, cos_b, sin_a, sin_b,
    x0, low, q_ext, k_ext, v_ext,
    table, weight, vec, wide,
):
    width = meta.shape[1]
    heads = q_ext.shape[0]
    model = x0.shape[0]
    vocab = embedding.shape[0]

    @pl.when(pl.program_id(0) == 0)
    def _():
        vec[...] = columns_of(vectors, wide)
        wide[...] = jnp.zeros_like(wide)
        for part, piece in enumerate(split3(embedding[...])):
            wide[part * THIRD : part * THIRD + vocab, :] = piece
        table[...] = wide[...].T.astype(bf16)
        for part in range(3):
            span = slice(part * model, (part + 1) * model)
            weight[span, :] = projection[:, span].astype(bf16).T

    ids = meta[0:1, :].astype(jnp.int32)
    vocab3 = rows_of(128, width)
    onehot = ((vocab3 == ids) | (vocab3 == ids + THIRD) | (vocab3 == ids + 2 * THIRD)).astype(f32).astype(bf16)
    embedded = dot(table[...], onehot)
    x0[...] = embedded
    hat, _ = norm_stats(embedded)
    normed = (hat * vec[:, 0:1] + vec[:, 1:2]).astype(bf16)
    row = rows_of(EXT - HEAD_DIM, width)
    low[0:model, :] = normed
    low[model : model + 16, :] = jnp.where(row == 0, 1.0, 0.0).astype(bf16)
    second = meta[2:3, :]
    in_second = second > 0.5
    cos = jnp.where(in_second, cos_a[...], cos_b[...])
    sin = jnp.where(in_second, sin_a[...], sin_b[...])
    q_rows = jnp.where(row == 0, second, jnp.where(row == 1, 1.0 - second, 0.0)).astype(bf16)
    k_rows = jnp.where(
        row == 0,
        -MASKED * (1.0 - second),
        jnp.where(row == 1, -MASKED * second, jnp.where(row < 5, 1.0, 0.0)),
    ).astype(bf16)
    v_rows = jnp.where(row < 3, 1.0, 0.0).astype(bf16)
    for part, out, extra in ((0, q_ext, q_rows), (1, k_ext, k_rows), (2, v_ext, v_rows)):
        base = part * model
        mixed = dot(weight[base : base + model, :], normed) + vec[:, 2 + part : 3 + part]
        for head in range(heads):
            one = mixed[head * HEAD_DIM : head * HEAD_DIM + HALF, :]
            two = mixed[head * HEAD_DIM + HALF : (head + 1) * HEAD_DIM, :]
            if part < 2:
                one, two = one * cos - two * sin, two * cos + one * sin
            out[head, 0:HALF, :] = one.astype(bf16)
            out[head, HALF:HEAD_DIM, :] = two.astype(bf16)
            out[head, HEAD_DIM:EXT, :] = extra


def attention_kernel(q_ext, k_ext, v_ext, out, q_next):
    heads, _, width = q_ext.shape
    factor = LOG2E * SCALE
    for head in range(heads):
        queries = q_ext[head]
        scores = dot(k_ext[head], queries, TN)
        top = jnp.max(scores, axis=0, keepdims=True)
        weights = jnp.exp2((scores - top) * factor).astype(bf16)
        mixed = dot(v_ext[head], weights)
        total = mixed[HEAD_DIM : HEAD_DIM + 1, :]
        out[head] = (mixed[0:HEAD_DIM, :] / total).astype(bf16)
        high, middle, rest = split3(-(top + jnp.log2(total) * (1.0 / factor)))
        q_next[head, 0:HEAD_DIM, :] = queries[0:HEAD_DIM, :]
        row = rows_of(EXT - HEAD_DIM, width)
        tail = queries[HEAD_DIM:EXT, :].astype(f32)
        tail = jnp.where(row == 2, high, jnp.where(row == 3, middle, jnp.where(row == 4, rest, tail)))
        q_next[head, HEAD_DIM:EXT, :] = tail.astype(bf16)


def attention_back_kernel(
    q_ext, k_ext, v_ext, do_ext, low, meta, cos_a, cos_b, sin_a, sin_b, *rest, chunk, chained
):
    dq, dk, dv, dweight, grads, total = rest[3:] if chained else rest
    slot = pl.program_id(0)
    heads, _, width = q_ext.shape
    in_second = meta[2:3, :] > 0.5
    cos = jnp.where(in_second, cos_a[...], cos_b[...])
    sin = jnp.where(in_second, sin_a[...], sin_b[...])
    for head in range(heads):
        keys = k_ext[head]
        q_parts = []
        k_total = v_total = None
        for at in range(0, width, chunk):
            piece = slice(at, at + chunk)
            queries, outs = q_ext[head, :, piece], do_ext[head, :, piece]
            prob = jnp.exp2(dot(queries, keys, TN) * (LOG2E * SCALE))
            inner = dot(outs, v_ext[head], TN)
            score_grad = (prob * inner).astype(bf16)
            q_parts.append(dot(keys[0:HEAD_DIM, :], score_grad, NT))
            k_part = dot(queries[0:HEAD_DIM, :], score_grad)
            v_part = dot(outs[0:HEAD_DIM, :], prob.astype(bf16))
            k_total = k_part if k_total is None else k_total + k_part
            v_total = v_part if v_total is None else v_total + v_part
        for part, (out, grad) in enumerate(((dq, jnp.concatenate(q_parts, axis=1)), (dk, k_total), (dv, v_total))):
            one, two = grad[0:HALF, :], grad[HALF:HEAD_DIM, :]
            if part < 2:
                one, two = one * SCALE, two * SCALE
                one, two = one * cos + two * sin, two * cos - one * sin
            out[head, 0:HALF, :] = one.astype(bf16)
            out[head, HALF:HEAD_DIM, :] = two.astype(bf16)
            base = (part * heads + head) * HEAD_DIM
            grads[base : base + HEAD_DIM, :] = out[head]
    share = dot(low[...], grads[...], NT)
    rows = share.shape[0]

    @pl.when(slot == 0)
    def _():
        total[...] = share

    @pl.when(slot > 0)
    def _():
        total[...] += share

    @pl.when(slot == pl.num_programs(0) - 1)
    def _():
        dweight[...] = jnp.zeros_like(dweight)
        dweight[0:rows, :] = total[...].astype(bf16)


def middle_kernel(
    meta, x0, attended, outward, w_up, w_down, embedding, vectors,
    dx1, do_ext, dw_pair, dw_rest, loss,
    up_t, down_t, act, slope, dw_up, dw_down, dw_out, dtable, dvec, vec, wide, table, table_t, w_out, w_out_t, sems,
):
    step = pl.program_id(0)
    chunks = w_up.shape[0]
    model, width = x0.shape
    heads = do_ext.shape[0]
    vocab = embedding.shape[0]

    @pl.when(step == 0)
    def _():
        for part in range(chunks):
            up_t[part] = w_up[part].T
            down_t[part] = w_down[part].T
        vec[...] = columns_of(vectors, wide)
        wide[...] = jnp.zeros_like(wide)
        wide[0:vocab, :] = embedding[...]
        table[...] = wide[0:VPAD, :].astype(bf16)
        table_t[...] = wide[...].T.astype(bf16)
        w_out[...] = outward[...].astype(bf16)
        w_out_t[...] = w_out[...].T
        dw_up[...] = jnp.zeros_like(dw_up)
        dw_down[...] = jnp.zeros_like(dw_down)
        dw_out[...] = jnp.zeros_like(dw_out)
        dtable[...] = jnp.zeros_like(dtable)
        dvec[...] = jnp.zeros_like(dvec)
        loss[...] = jnp.zeros_like(loss)

    def col(index):
        return vec[:, index : index + 1]

    after = 8 + chunks_of_bias(model)
    x1 = x0[...] + dot(w_out_t[...], attended[...]) + col(5)
    hat_two, inverse_two = norm_stats(x1)
    c_low = (hat_two * col(6) + col(7)).astype(bf16)
    branch = None
    for part in range(chunks):
        hidden = dot(up_t[part], c_low) + col(8 + part)
        cdf = 0.5 + 0.5 * lax.erf(hidden * (0.5**0.5))
        density = jnp.exp(hidden * hidden * -0.5) * (1.0 / math.sqrt(2.0 * math.pi))
        act[part] = (hidden * cdf).astype(bf16)
        slope[part] = (cdf + hidden * density).astype(bf16)
        share = dot(w_down[part], act[part])
        branch = share if branch is None else branch + share
    x2 = x1 + branch + col(after)
    hat_end, inverse_end = norm_stats(x2)
    f_low = (hat_end * col(after + 1) + col(after + 2)).astype(bf16)
    vocab_rows = rows_of(VPAD, width)
    logits = jnp.where(vocab_rows < vocab, dot(table[...], f_low), -MASKED)
    top = jnp.max(logits, axis=0, keepdims=True)
    raised = jnp.exp(logits - top)
    total = jnp.sum(raised, axis=0, keepdims=True)
    target = (vocab_rows == meta[1:2, :].astype(jnp.int32)).astype(f32)
    chosen = jnp.sum(logits * target, axis=0, keepdims=True)
    weight = meta[3:4, :]
    loss[0:1, :] += jnp.broadcast_to(lane_sum(weight * (jnp.log(total) + top - chosen)), (1, loss.shape[1]))
    logit_grad = (weight * (raised / total - target)).astype(bf16)
    dtable[...] += dot(logit_grad, f_low, NT)
    f_grad = dot(table_t[:, 0:VPAD], logit_grad)
    dvec[:, 4 + chunks : 5 + chunks] += lane_sum(f_grad * hat_end)
    dvec[:, 5 + chunks : 6 + chunks] += lane_sum(f_grad)
    x2_grad = norm_back(f_grad, hat_end, inverse_end, col(after + 1))
    g_low = x2_grad.astype(bf16)
    dvec[:, 3 + chunks : 4 + chunks] += lane_sum(g_low.astype(f32))
    c_grad = None
    for part in range(chunks):
        hidden_grad = (dot(down_t[part], g_low) * slope[part]).astype(bf16)
        dw_up[part] += dot(c_low, hidden_grad, NT)
        dw_down[part] += dot(g_low, act[part], NT)
        dvec[:, 3 + part : 4 + part] += lane_sum(hidden_grad.astype(f32))
        share = dot(w_up[part], hidden_grad)
        c_grad = share if c_grad is None else c_grad + share
    dvec[:, 1:2] += lane_sum(c_grad * hat_two)
    dvec[:, 2:3] += lane_sum(c_grad)
    x1_grad = x2_grad + norm_back(c_grad, hat_two, inverse_two, col(6))
    dx1[...] = x1_grad
    x1_low = x1_grad.astype(bf16)
    dvec[:, 0:1] += lane_sum(x1_low.astype(f32))
    dw_out[...] += dot(attended[...], x1_low, NT)
    o_grad = dot(w_out[...], x1_low).astype(bf16)
    inner = o_grad.astype(f32) * attended[...].astype(f32)
    row = rows_of(EXT - HEAD_DIM, width)
    for head in range(heads):
        span = slice(head * HEAD_DIM, (head + 1) * HEAD_DIM)
        high, middle, rest = split3(-jnp.sum(inner[span, :], axis=0, keepdims=True))
        do_ext[head, 0:HEAD_DIM, :] = o_grad[span, :]
        tail = jnp.where(row == 0, high, jnp.where(row == 1, middle, jnp.where(row == 2, rest, 0.0)))
        do_ext[head, HEAD_DIM:EXT, :] = tail.astype(bf16)

    @pl.when(step == pl.num_programs(0) - 1)
    def _():
        copies = []
        for side, (low, grad) in enumerate(((up_t, dw_up), (down_t, dw_down))):
            low[...] = grad[...].astype(bf16)
            copies.append(pltpu.make_async_copy(low, dw_pair.at[side], sems.at[side]))
            copies[side].start()
        dw_rest[...] = jnp.zeros_like(dw_rest)
        dw_rest[0:model, :] = dw_out[...].astype(bf16)
        wide[...] = dvec[...].T
        wide[REST_TABLE : REST_TABLE + VPAD, :] = dtable[...]
        dw_rest[model : model + 128, :] = wide[...].astype(bf16)
        for copy in copies:
            copy.wait()


def chunks_of_bias(model):
    return FF // model


def input_back_kernel(meta, x0, dq, dk, dv, dx1, projection, vectors, rest, weight, vec, wide, dvec, dtable):
    step = pl.program_id(0)
    model, width = x0.shape

    @pl.when(step == 0)
    def _():
        vec[...] = columns_of(vectors, wide)
        weight[...] = projection[...].astype(bf16)
        dtable[...] = jnp.zeros_like(dtable)
        dvec[...] = jnp.zeros_like(dvec)

    back = None
    for part, grad in enumerate((dq, dk, dv)):
        share = dot(weight[:, part * model : (part + 1) * model], grad[...])
        back = share if back is None else back + share
    hat, inverse = norm_stats(x0[...])
    dvec[:, VPAD : VPAD + 1] += lane_sum(back * hat)
    dvec[:, VPAD + 1 : VPAD + 2] += lane_sum(back)
    x0_grad = dx1[...] + norm_back(back, hat, inverse, vec[:, 0:1])
    onehot = (rows_of(VPAD, width) == meta[0:1, :].astype(jnp.int32)).astype(f32).astype(bf16)
    for piece in split3(x0_grad):
        dtable[...] += dot(onehot, piece.astype(bf16), NT)

    @pl.when(step == pl.num_programs(0) - 1)
    def _():
        wide[...] = dvec[...].T
        rest[0:VPAD, :] = dtable[...]
        rest[VPAD:, :] = wide[VPAD : VPAD + 8, :]


def whole(shape):
    return pl.BlockSpec(shape, lambda *_: (0,) * len(shape), pipeline_mode=pl.Buffered(1))


def shaped(shape, dtype):
    return jax.ShapeDtypeStruct(shape, dtype)


def limits(mib):
    return pltpu.CompilerParams(vmem_limit_bytes=mib * MIB)


def cost(flops, moved, transcendentals=0):
    return pl.CostEstimate(flops=int(flops), bytes_accessed=int(moved), transcendentals=int(transcendentals))


def adam_step(weight, grad, drift, spread, rate):
    drift = FIRST_DECAY * drift + (1.0 - FIRST_DECAY) * grad
    spread = SECOND_DECAY * spread + (1.0 - SECOND_DECAY) * grad * grad
    adjusted = (
        drift
        / (1.0 - FIRST_DECAY**STEP)
        / (jnp.sqrt(spread / (1.0 - SECOND_DECAY**STEP)) + ADAM_EPS)
    )
    return (weight - rate * (adjusted + WEIGHT_DECAY * weight), drift, spread)


def rotary_constants(rows):
    freq = np.float32(10000.0) ** (-np.arange(0, HEAD_DIM, 2, dtype=np.float32) / np.float32(HEAD_DIM))
    angle = np.arange(rows, dtype=np.float32)[None, :] * freq[:, None].astype(np.float32)
    return np.cos(angle).astype(np.float32), np.sin(angle).astype(np.float32)


def body(
    columns,
    deep,
    true_ids,
    picked,
    replace_kinds,
    random_ids,
    splits,
    embedding,
    projection,
    outward,
    feedforward,
    vectors,
    embedding_drift,
    embedding_spread,
    projection_drift,
    projection_spread,
    outward_drift,
    outward_spread,
    feedforward_drift,
    feedforward_spread,
    vectors_drift,
    vectors_spread,
):
    tokens = true_ids.shape[0]
    slots = splits.shape[0]
    rows = tokens // slots
    half = rows // 2
    vocab, model = embedding.shape
    heads = model // HEAD_DIM
    bias_rows = chunks_of_bias(model)
    block = half
    blocks = tokens // block
    wide = FF // columns
    devices = columns * deep * 2
    chips = ("col", "deep")
    everywhere = ("col", "deep", "core")

    pair_all = lax.all_gather(feedforward.astype(bf16), everywhere, axis=1, tiled=True)
    pair_all = pair_all.reshape(2, columns, model, wide)

    masked = (picked == 1) & (replace_kinds < 8)
    swapped = (picked == 1) & (replace_kinds == 8)
    input_ids = jnp.where(masked, MASK_ID, jnp.where(swapped, random_ids, true_ids))
    within = jnp.arange(rows, dtype=jnp.int32)
    second = ((within[None, :] >= half).astype(jnp.int32) * splits[:, None]).astype(f32)
    pick = picked.astype(f32).reshape(slots, rows)
    half_counts = jnp.sum(pick.reshape(slots, 2, half), axis=2)
    split = splits[:, None].astype(f32)
    half_counts = jnp.where(split > 0.5, half_counts, jnp.sum(half_counts, axis=1, keepdims=True))
    token_weight = (pick.reshape(slots, 2, half) / half_counts[:, :, None]).reshape(tokens)
    zero = jnp.zeros((tokens,), f32)
    meta = jnp.stack(
        [input_ids.astype(f32), true_ids.astype(f32), second.reshape(-1), token_weight, zero, zero, zero, zero]
    )
    cos_np, sin_np = rotary_constants(rows)
    cos_table, sin_table = jnp.asarray(cos_np), jnp.asarray(sin_np)
    twice_cos, twice_sin = (jnp.asarray(np.tile(t[:, :half], (1, 2))) for t in (cos_np, sin_np))

    def by_block(count):
        return pl.BlockSpec((count, block), lambda i: (0, i))

    def heads_block(count):
        return pl.BlockSpec((heads, count, block), lambda i: (0, 0, i))

    first_half = pl.BlockSpec((HALF, block), lambda i: (0, 0))
    own_half = pl.BlockSpec((HALF, block), lambda i: (0, i % 2))
    x0, normed, q_ext, k_ext, v_ext = pl.pallas_call(
        qkv_kernel,
        grid=(blocks,),
        in_specs=[by_block(8), whole((vocab, model)), whole((model, 3 * model)), whole(vectors.shape),
                  first_half, own_half, first_half, own_half],
        out_specs=[by_block(model), by_block(model + 16), heads_block(EXT), heads_block(EXT), heads_block(EXT)],
        out_shape=[shaped((model, tokens), f32), shaped((model + 16, tokens), bf16)]
        + [shaped((heads, EXT, tokens), bf16)] * 3,
        scratch_shapes=[pltpu.VMEM((model, 128), bf16), pltpu.VMEM((3 * model, model), bf16), pltpu.VMEM((model, 128), f32),
                        pltpu.VMEM((128, model), f32)],
        compiler_params=limits(56),
        cost_estimate=cost(2 * 3 * model * model * tokens, 20 * model * tokens),
        name="embed_and_qkv",
    )(meta, embedding, projection, vectors, cos_table, cos_table, sin_table, sin_table)

    per = 4

    def head_group(count, size, first=0):
        return pl.BlockSpec((size, count, rows), lambda s, g: (first + g, 0, s))

    attended, q_next = pl.pallas_call(
        attention_kernel,
        grid=(slots, heads // per),
        in_specs=[head_group(EXT, per)] * 3,
        out_specs=[head_group(HEAD_DIM, per), head_group(EXT, per)],
        out_shape=[shaped((heads, HEAD_DIM, tokens), bf16), shaped((heads, EXT, tokens), bf16)],
        compiler_params=limits(56),
        cost_estimate=cost(2 * 16 * model * rows * tokens, 12 * model * tokens, heads * rows * tokens),
        name="attention",
    )(q_ext, k_ext, v_ext)
    attended = attended.reshape(model, tokens)

    shard = -(-(model + 128) // devices)
    shard = -(-shard // 8) * 8
    padded = shard * devices
    dx1, do_ext, dw_pair, dw_rest, loss = pl.pallas_call(
        middle_kernel,
        grid=(blocks,),
        in_specs=[by_block(8), by_block(model), by_block(model), whole((model, model)),
                  pl.BlockSpec((None, columns, model, wide), lambda i: (0, 0, 0, 0), pipeline_mode=pl.Buffered(1)),
                  pl.BlockSpec((None, columns, model, wide), lambda i: (1, 0, 0, 0), pipeline_mode=pl.Buffered(1)),
                  whole((vocab, model)), whole(vectors.shape)],
        out_specs=[by_block(model), heads_block(EXT), pl.BlockSpec(memory_space=pl.ANY), whole((model + 128, model)), whole((8, 128))],
        out_shape=[shaped((model, tokens), f32), shaped((heads, EXT, tokens), bf16), shaped((2, columns, model, wide), bf16),
                   shaped((model + 128, model), bf16), shaped((8, 128), f32)],
        scratch_shapes=[pltpu.VMEM((columns, wide, model), bf16), pltpu.VMEM((columns, wide, model), bf16),
                        pltpu.VMEM((columns, wide, block), bf16), pltpu.VMEM((columns, wide, block), bf16),
                        pltpu.VMEM((columns, model, wide), f32), pltpu.VMEM((columns, model, wide), f32),
                        pltpu.VMEM((model, model), f32), pltpu.VMEM((VPAD, model), f32), pltpu.VMEM((model, 128), f32),
                        pltpu.VMEM((model, 128), f32), pltpu.VMEM((128, model), f32),
                        pltpu.VMEM((VPAD, model), bf16), pltpu.VMEM((model, 128), bf16),
                        pltpu.VMEM((model, model), bf16), pltpu.VMEM((model, model), bf16), pltpu.SemaphoreType.DMA((2,))],
        compiler_params=limits(62),
        cost_estimate=cost(2 * tokens * model * (6 * FF + 3 * model), 14 * model * tokens + 16 * model * FF, FF * tokens),
        name="feedforward_and_head",
    )(meta, x0, attended, outward, pair_all, pair_all, embedding, vectors)

    def swap(values, axes):
        return lax.all_to_all(values, axes, 0, 0, tiled=True)

    def add_up(values, pieces):
        return jnp.sum(values.reshape((pieces, -1) + values.shape[1:]).astype(f32), axis=0)

    def pad_rows(values):
        return jnp.pad(values, ((0, padded - values.shape[0]), (0, 0))) if padded > values.shape[0] else values

    def reduce_core(values):
        return add_up(swap(values, "core"), 2).astype(bf16)

    def spread(values, axes, count):
        return swap(jnp.broadcast_to(values[None], (count,) + values.shape).reshape((-1,) + values.shape[1:]), axes)

    pair = dw_pair.reshape(2 * columns * model, wide)
    pair = reduce_core(pair)
    pair = add_up(swap(pair, "col"), columns).astype(bf16)
    pair = add_up(swap(pair, "deep"), deep)
    pair_grad = swap(pair, "core").reshape(feedforward.shape)

    def to_owner(values):
        return add_up(swap(values, chips), columns * deep).astype(bf16)

    def to_chips(values):
        return spread(values, chips, columns * deep)

    rest_mine = reduce_core(pad_rows(dw_rest))
    rest_mine = to_chips(to_owner(rest_mine))

    per_call = 4
    width = 3 * per_call * HEAD_DIM
    grads = None
    in_parts = []
    for first in range(0, heads // per_call):
        chained = grads is not None

        def group(count, first=first):
            return pl.BlockSpec((per_call, count, rows), lambda s: (first, 0, s))

        table_spec = pl.BlockSpec((HALF, rows), lambda s: (0, 0))
        outs = pl.pallas_call(
            functools.partial(attention_back_kernel, chunk=half, chained=chained),
            grid=(slots,),
            in_specs=[group(EXT)] * 4
            + [pl.BlockSpec((model + 16, rows), lambda s: (0, s)), pl.BlockSpec((8, rows), lambda s: (0, s))]
            + [table_spec] * 4
            + [pl.BlockSpec(memory_space=pl.ANY)] * (3 if chained else 0),
            out_specs=[group(HEAD_DIM)] * 3 + [pl.BlockSpec((model + 128, width), lambda s: (0, 0))],
            out_shape=[shaped((heads, HEAD_DIM, tokens), bf16)] * 3 + [shaped((model + 128, width), bf16)],
            scratch_shapes=[pltpu.VMEM((width, rows), bf16), pltpu.VMEM((model + 16, width), f32)],
            input_output_aliases={10: 0, 11: 1, 12: 2} if chained else {},
            compiler_params=limits(56),
            cost_estimate=cost(2 * 40 * width // 3 * rows * tokens, 20 * width * tokens, per_call * rows * tokens),
            name="attention_back",
        )(q_next, k_ext, v_ext, do_ext, normed, meta, twice_cos, cos_table, twice_sin, sin_table, *(grads or ()))
        grads = outs[:3]
        in_parts.append(pad_rows(outs[3]))
    dq, dk, dv = (grad.reshape(model, tokens) for grad in grads)
    early = len(in_parts) - 2
    in_mine = []
    for parts in (in_parts[:early], in_parts[early:]):
        merged = jnp.concatenate([reduce_core(part) for part in parts], axis=1)
        in_mine.append(to_chips(to_owner(merged)))
    in_mine = jnp.concatenate(in_mine, axis=1)

    rest_start = pl.pallas_call(
        input_back_kernel,
        grid=(blocks,),
        in_specs=[by_block(8)] + [by_block(model)] * 5 + [whole((model, 3 * model)), whole(vectors.shape)],
        out_specs=whole((VPAD + 8, model)),
        out_shape=shaped((VPAD + 8, model), f32),
        scratch_shapes=[pltpu.VMEM((model, 3 * model), bf16), pltpu.VMEM((model, 128), f32), pltpu.VMEM((128, model), f32),
                        pltpu.VMEM((model, 128), f32), pltpu.VMEM((VPAD, model), f32)],
        compiler_params=limits(56),
        cost_estimate=cost(2 * 3 * model * model * tokens, 20 * model * tokens),
        name="input_back",
    )(meta, x0, dq, dk, dv, dx1, projection, vectors)

    scalars = jnp.stack([loss[0, 0], jnp.sum(1 + splits).astype(f32), jnp.sum(pair_grad * pair_grad)])
    late = jnp.concatenate([rest_start, jnp.pad(scalars[None], ((0, 7), (0, model - 3)))], axis=0)
    size = 1
    while size < devices:
        late = late + lax.ppermute(late, everywhere, [(i, i ^ size) for i in range(devices)])
        size *= 2
    loss_total, crops, ffn_total = late[VPAD + 8, 0], late[VPAD + 8, 1], late[VPAD + 8, 2]

    full = spread(jnp.concatenate([in_mine, rest_mine], axis=1), "core", 2).astype(f32)
    groups = heads // per_call
    piece = per_call * HEAD_DIM
    in_full = jnp.concatenate(
        [full[: model + 8, g * width + part * piece : g * width + (part + 1) * piece] for part in range(3) for g in range(groups)],
        axis=1,
    )
    rest_full = full[: model + 128, groups * width :]
    in_grad = in_full[:model]
    out_grad = rest_full[:model]
    table_grad = rest_full[model + REST_TABLE : model + REST_TABLE + vocab] + late[:vocab]
    vector_grad = jnp.concatenate(
        [late[VPAD : VPAD + 2], in_full[model].reshape(3, model), rest_full[model : model + 6 + bias_rows]], axis=0
    )
    rep_grads = (table_grad, in_grad, out_grad, vector_grad)
    squares = ffn_total
    for grad in rep_grads:
        squares = squares + jnp.sum(grad * grad)
    share = 1.0 / crops
    grad_norm = jnp.sqrt(squares) * share
    factor = jnp.minimum(1.0, CLIP_NORM / (grad_norm + 1e-06)) * share
    replicated = (embedding, projection, outward, vectors)
    drifts = (embedding_drift, projection_drift, outward_drift, vectors_drift)
    spreads = (embedding_spread, projection_spread, outward_spread, vectors_spread)
    rep_out = [
        adam_step(weight, grad * factor, drift, spread, rate)
        for weight, grad, drift, spread, rate in zip(replicated, rep_grads, drifts, spreads, (0.05, 0.05, 0.1, 0.2))
    ]
    ffn_out = adam_step(feedforward, pair_grad * factor, feedforward_drift, feedforward_spread, 0.05)
    results = [jnp.stack([loss_total, crops]), grad_norm]
    for fresh, moved, varied in (rep_out[0], rep_out[1], rep_out[2], ffn_out, rep_out[3]):
        results.extend([fresh, moved, varied, fresh.astype(bf16)])
    return tuple(results)


def solution(mesh):
    columns, row = mesh.shape["col"], mesh.shape["row"]
    fine = jax.sharding.Mesh(mesh.devices.reshape(columns, row // 2, 2), ("col", "deep", "core"))
    split_all, tiles, full = P(("col", "deep", "core")), P(None, ("deep", "core"), "col"), P()
    return jax.shard_map(
        functools.partial(body, columns, row // 2),
        mesh=fine,
        in_specs=(split_all,) * 5 + (full,) * 3 + (tiles,) + (full,) * 7 + (tiles,) * 2 + (full,) * 2,
        out_specs=(full,) * 14 + (tiles,) * 4 + (full,) * 4,
        check_vma=False,
    )
```

```python
import functools
import math

import jax
import jax.numpy as jnp
import numpy as np
from jax import lax
from jax.experimental import pallas as pl
from jax.experimental.pallas import tpu as pltpu
from jax.sharding import PartitionSpec as P

HEAD_DIM = 32
HALF = HEAD_DIM // 2
EXT = HEAD_DIM + 16
FF = 2560
STEP = 10
VPAD = 48
VOCAB_ROWS = 40
TAIL = 24
UNITS = 1280
THIRD = 40
REST_TABLE = 32

EPS_NORM = 1e-05
CLIP_NORM = 0.002
FIRST_DECAY = 0.5
SECOND_DECAY = 0.5
ADAM_EPS = 1e-08
WEIGHT_DECAY = 0.01
MASK_ID = 32
MASKED = 1e30

LOG2E = math.log2(math.e)
SCALE = HEAD_DIM ** (-0.5)
MIB = 2**20

bf16 = jnp.bfloat16
f32 = jnp.float32

NN = ((1,), (0,))
NT = ((1,), (1,))
TN = ((0,), (0,))


def dot(left, right, dims=NN):
    return lax.dot_general(left, right, (dims, ((), ())), preferred_element_type=f32)


def split3(values):
    high = values.astype(bf16).astype(f32)
    rest = values - high
    middle = rest.astype(bf16).astype(f32)
    return high, middle, rest - middle


def norm_stats(values):
    center = values - jnp.mean(values, axis=0, keepdims=True)
    inverse = lax.rsqrt(jnp.mean(center * center, axis=0, keepdims=True) + EPS_NORM)
    return center * inverse, inverse


def norm_back(grad, hat, inverse, gain):
    scaled = grad * gain
    return inverse * (
        scaled
        - jnp.mean(scaled, axis=0, keepdims=True)
        - hat * jnp.mean(scaled * hat, axis=0, keepdims=True)
    )


def rows_of(count, width):
    return lax.broadcasted_iota(jnp.int32, (count, width), 0)


def split_halves(total, keep, send):
    rows = keep.shape[0]
    first, second = total[0:rows, :], total[rows:, :]
    is_first = lax.axis_index("core") == 0
    keep[...] = jnp.where(is_first, first, second).astype(bf16)
    send[...] = jnp.where(is_first, second, first).astype(bf16)


def lane_sum(values):
    return jnp.sum(values, axis=1, keepdims=True)


def columns_of(vectors, wide):
    wide[...] = jnp.zeros_like(wide)
    wide[0 : vectors.shape[0], :] = vectors[...]
    return wide[...].T


def qkv_kernel(
    meta, embedding, projection, vectors, cos_a, cos_b, sin_a, sin_b,
    x0, low, q_ext, k_ext, v_ext,
    table, weight, vec, wide,
):
    width = meta.shape[1]
    heads = q_ext.shape[0]
    model = x0.shape[0]
    vocab = embedding.shape[0]

    @pl.when(pl.program_id(0) == 0)
    def _():
        vec[...] = columns_of(vectors, wide)
        wide[...] = jnp.zeros_like(wide)
        for part, piece in enumerate(split3(embedding[...])):
            wide[part * THIRD : part * THIRD + vocab, :] = piece
        table[...] = wide[...].T.astype(bf16)
        for part in range(3):
            span = slice(part * model, (part + 1) * model)
            weight[span, :] = projection[:, span].astype(bf16).T

    ids = meta[0:1, :].astype(jnp.int32)
    vocab3 = rows_of(128, width)
    onehot = ((vocab3 == ids) | (vocab3 == ids + THIRD) | (vocab3 == ids + 2 * THIRD)).astype(f32).astype(bf16)
    embedded = dot(table[...], onehot)
    x0[...] = embedded
    hat, _ = norm_stats(embedded)
    normed = (hat * vec[:, 0:1] + vec[:, 1:2]).astype(bf16)
    row = rows_of(EXT - HEAD_DIM, width)
    low[0:model, :] = normed
    low[model : model + 16, :] = jnp.where(row == 0, 1.0, 0.0).astype(bf16)
    second = meta[2:3, :]
    in_second = second > 0.5
    cos = jnp.where(in_second, cos_a[...], cos_b[...])
    sin = jnp.where(in_second, sin_a[...], sin_b[...])
    q_rows = jnp.where(row == 0, second, jnp.where(row == 1, 1.0 - second, 0.0)).astype(bf16)
    k_rows = jnp.where(
        row == 0,
        -MASKED * (1.0 - second),
        jnp.where(row == 1, -MASKED * second, jnp.where(row < 5, 1.0, 0.0)),
    ).astype(bf16)
    v_rows = jnp.where(row < 3, 1.0, 0.0).astype(bf16)
    for part, out, extra in ((0, q_ext, q_rows), (1, k_ext, k_rows), (2, v_ext, v_rows)):
        base = part * model
        mixed = dot(weight[base : base + model, :], normed) + vec[:, 2 + part : 3 + part]
        for head in range(heads):
            one = mixed[head * HEAD_DIM : head * HEAD_DIM + HALF, :]
            two = mixed[head * HEAD_DIM + HALF : (head + 1) * HEAD_DIM, :]
            if part < 2:
                one, two = one * cos - two * sin, two * cos + one * sin
            out[head, 0:HALF, :] = one.astype(bf16)
            out[head, HALF:HEAD_DIM, :] = two.astype(bf16)
            out[head, HEAD_DIM:EXT, :] = extra


def attention_kernel(q_ext, k_ext, v_ext, out, q_next):
    heads, _, width = q_ext.shape
    factor = LOG2E * SCALE
    upcoming = dot(k_ext[0], q_ext[0], TN)
    for head in range(heads):
        queries = q_ext[head]
        scores = upcoming
        if head + 1 < heads:
            upcoming = dot(k_ext[head + 1], q_ext[head + 1], TN)
        top = jnp.max(scores, axis=0, keepdims=True)
        weights = jnp.exp2((scores - top) * factor).astype(bf16)
        mixed = dot(v_ext[head], weights)
        total = mixed[HEAD_DIM : HEAD_DIM + 1, :]
        out[head] = (mixed[0:HEAD_DIM, :] / total).astype(bf16)
        high, middle, rest = split3(-(top + jnp.log2(total) * (1.0 / factor)))
        q_next[head, 0:HEAD_DIM, :] = queries[0:HEAD_DIM, :]
        row = rows_of(EXT - HEAD_DIM, width)
        tail = queries[HEAD_DIM:EXT, :].astype(f32)
        tail = jnp.where(row == 2, high, jnp.where(row == 3, middle, jnp.where(row == 4, rest, tail)))
        q_next[head, HEAD_DIM:EXT, :] = tail.astype(bf16)


def attention_back_kernel(
    q_ext, k_ext, v_ext, do_ext, low, meta, cos_a, cos_b, sin_a, sin_b, *rest, chunk, chained
):
    dq, dk, dv, keep, send, grads, total = rest[3:] if chained else rest
    slot = pl.program_id(0)
    heads, _, width = q_ext.shape
    in_second = meta[2:3, :] > 0.5
    cos = jnp.where(in_second, cos_a[...], cos_b[...])
    sin = jnp.where(in_second, sin_a[...], sin_b[...])
    for head in range(heads):
        keys = k_ext[head]
        q_parts = []
        k_total = v_total = None
        for at in range(0, width, chunk):
            piece = slice(at, at + chunk)
            queries, outs = q_ext[head, :, piece], do_ext[head, :, piece]
            prob = jnp.exp2(dot(queries, keys, TN) * (LOG2E * SCALE))
            inner = dot(outs, v_ext[head], TN)
            score_grad = (prob * inner).astype(bf16)
            q_parts.append(dot(keys[0:HEAD_DIM, :], score_grad, NT))
            k_part = dot(queries[0:HEAD_DIM, :], score_grad)
            v_part = dot(outs[0:HEAD_DIM, :], prob.astype(bf16))
            k_total = k_part if k_total is None else k_total + k_part
            v_total = v_part if v_total is None else v_total + v_part
        for part, (out, grad) in enumerate(((dq, jnp.concatenate(q_parts, axis=1)), (dk, k_total), (dv, v_total))):
            one, two = grad[0:HALF, :], grad[HALF:HEAD_DIM, :]
            if part < 2:
                one, two = one * SCALE, two * SCALE
                one, two = one * cos + two * sin, two * cos - one * sin
            out[head, 0:HALF, :] = one.astype(bf16)
            out[head, HALF:HEAD_DIM, :] = two.astype(bf16)
            base = (part * heads + head) * HEAD_DIM
            grads[base : base + HEAD_DIM, :] = out[head]
    share = dot(low[...], grads[...], NT)
    rows = share.shape[0]

    @pl.when(slot == 0)
    def _():
        total[0:rows, :] = share

    @pl.when(slot > 0)
    def _():
        total[0:rows, :] += share

    @pl.when(slot == pl.num_programs(0) - 1)
    def _():
        half_rows = keep.shape[0]
        total[rows:, :] = jnp.zeros((2 * half_rows - rows, total.shape[1]), f32)
        split_halves(total, keep, send)


def middle_kernel(
    meta, x0, attended, outward, pair_all, embedding, vectors,
    dx1, do_ext, keep_pair, send_pair, keep_rest, send_rest, loss,
    w_up, w_down, up_t, down_t, act, slope, dw_up, dw_down, dw_out, dtable, dvec, vec, wide, table, table_t, w_out, w_out_t,
    sems,
):
    step = pl.program_id(0)
    chunks = pair_all.shape[1]
    model, width = x0.shape
    hidden_units = w_up.shape[1]
    unit = hidden_units // chunks
    heads = do_ext.shape[0]
    vocab = embedding.shape[0]

    @pl.when(step == 0)
    def _():
        fetches = []
        for side, into in enumerate((w_up, w_down)):
            for part in range(chunks):
                fetch = pltpu.make_async_copy(
                    pair_all.at[side, part], into.at[:, pl.ds(part * unit, unit)], sems.at[2 + side * chunks + part]
                )
                fetch.start()
                fetches.append(fetch)
        vec[...] = columns_of(vectors, wide)
        wide[...] = jnp.zeros_like(wide)
        wide[0:vocab, :] = embedding[...]
        table[...] = wide[0:VPAD, :].astype(bf16)
        table_t[...] = wide[...].T.astype(bf16)
        w_out[...] = outward[...].astype(bf16)
        w_out_t[...] = w_out[...].T
        dw_up[...] = jnp.zeros_like(dw_up)
        dw_down[...] = jnp.zeros_like(dw_down)
        dw_out[...] = jnp.zeros_like(dw_out)
        dtable[...] = jnp.zeros_like(dtable)
        dvec[...] = jnp.zeros_like(dvec)
        loss[...] = jnp.zeros_like(loss)
        for fetch in fetches:
            fetch.wait()
        for part in range(chunks):
            span = slice(part * unit, (part + 1) * unit)
            up_t[span, :] = w_up[:, span].T
            down_t[span, :] = w_down[:, span].T

    def col(index):
        return vec[:, index : index + 1]

    after = 8 + chunks_of_bias(model)
    x1 = x0[...] + dot(w_out_t[...], attended[...]) + col(5)
    hat_two, inverse_two = norm_stats(x1)
    c_low = (hat_two * col(6) + col(7)).astype(bf16)
    for first in range(0, hidden_units, UNITS):
        inner = dot(up_t[first : first + UNITS, :], c_low)
        for at in range(first, first + UNITS, model):
            hidden = inner[at - first : at - first + model, :] + col(8 + at // model)
            cdf = 0.5 + 0.5 * lax.erf(hidden * (0.5**0.5))
            density = jnp.exp(hidden * hidden * -0.5) * (1.0 / math.sqrt(2.0 * math.pi))
            act[at : at + model, :] = (hidden * cdf).astype(bf16)
            slope[at : at + model, :] = (cdf + hidden * density).astype(bf16)
    x2 = x1 + dot(w_down[...], act[...]) + col(after)
    hat_end, inverse_end = norm_stats(x2)
    f_low = (hat_end * col(after + 1) + col(after + 2)).astype(bf16)
    vocab_rows = rows_of(VPAD, width)
    logits = jnp.where(vocab_rows < vocab, dot(table[...], f_low), -MASKED)
    top = jnp.max(logits, axis=0, keepdims=True)
    raised = jnp.exp(logits - top)
    total = jnp.sum(raised, axis=0, keepdims=True)
    target = (vocab_rows == meta[1:2, :].astype(jnp.int32)).astype(f32)
    chosen = jnp.sum(logits * target, axis=0, keepdims=True)
    weight = meta[3:4, :]
    loss[0:1, :] += jnp.broadcast_to(lane_sum(weight * (jnp.log(total) + top - chosen)), (1, loss.shape[1]))
    logit_grad = (weight * (raised / total - target)).astype(bf16)
    dtable[...] += dot(logit_grad, f_low, NT)
    f_grad = dot(table_t[:, 0:VPAD], logit_grad)
    dvec[:, 4 + chunks : 5 + chunks] += lane_sum(f_grad * hat_end)
    dvec[:, 5 + chunks : 6 + chunks] += lane_sum(f_grad)
    x2_grad = norm_back(f_grad, hat_end, inverse_end, col(after + 1))
    g_low = x2_grad.astype(bf16)
    dvec[:, 3 + chunks : 4 + chunks] += lane_sum(g_low.astype(f32))
    dw_down[...] += dot(g_low, act[...], NT)
    for first in range(0, hidden_units, UNITS):
        span = slice(first, first + UNITS)
        act[span, :] = (dot(down_t[span, :], g_low) * slope[span, :]).astype(bf16)
    c_grad = dot(w_up[...], act[...])
    dw_up[...] += dot(c_low, act[...], NT)
    for part in range(hidden_units // model):
        dvec[:, 3 + part : 4 + part] += lane_sum(act[part * model : (part + 1) * model, :].astype(f32))
    dvec[:, 1:2] += lane_sum(c_grad * hat_two)
    dvec[:, 2:3] += lane_sum(c_grad)
    x1_grad = x2_grad + norm_back(c_grad, hat_two, inverse_two, col(6))
    dx1[...] = x1_grad
    x1_low = x1_grad.astype(bf16)
    dvec[:, 0:1] += lane_sum(x1_low.astype(f32))
    dw_out[0:model, :] += dot(attended[...], x1_low, NT)
    o_grad = dot(w_out[...], x1_low).astype(bf16)
    inner = o_grad.astype(f32) * attended[...].astype(f32)
    row = rows_of(EXT - HEAD_DIM, width)
    for head in range(heads):
        span = slice(head * HEAD_DIM, (head + 1) * HEAD_DIM)
        high, middle, rest = split3(-jnp.sum(inner[span, :], axis=0, keepdims=True))
        do_ext[head, 0:HEAD_DIM, :] = o_grad[span, :]
        tail = jnp.where(row == 0, high, jnp.where(row == 1, middle, jnp.where(row == 2, rest, 0.0)))
        do_ext[head, HEAD_DIM:EXT, :] = tail.astype(bf16)

    @pl.when(step == pl.num_programs(0) - 1)
    def _():
        is_first = lax.axis_index("core") == 0
        copies = []
        for side, (low, here, there, out) in enumerate(
            ((down_t, dw_down, dw_up, send_pair), (up_t, dw_up, dw_down, keep_pair))
        ):
            for part in range(chunks):
                span = slice(part * unit, (part + 1) * unit)
                low[part * model : (part + 1) * model, :] = jnp.where(is_first, here[:, span], there[:, span]).astype(bf16)
            copies.append(pltpu.make_async_copy(low, out, sems.at[side]))
            copies[side].start()
        wide[...] = dvec[...].T
        wide[REST_TABLE : REST_TABLE + VPAD, :] = dtable[...]
        dw_out[model:, :] = wide[...]
        split_halves(dw_out, keep_rest, send_rest)
        for copy in copies:
            copy.wait()


def chunks_of_bias(model):
    return FF // model


def input_back_kernel(meta, x0, dq, dk, dv, dx1, projection, vectors, *rest, last):
    if last:
        loss, dvec_in, dtable_in, tail, weight, vec, wide, dvec, dtable = rest
    else:
        dvec, dtable, weight, vec, wide = rest
    step = pl.program_id(0)
    model, width = x0.shape

    @pl.when(step == 0)
    def _():
        vec[...] = columns_of(vectors, wide)
        weight[...] = projection[...].astype(bf16)
        dtable[...] = dtable_in[...] if last else jnp.zeros_like(dtable)
        dvec[...] = dvec_in[...] if last else jnp.zeros_like(dvec)

    back = None
    for part, grad in enumerate((dq, dk, dv)):
        share = dot(weight[:, part * model : (part + 1) * model], grad[...])
        back = share if back is None else back + share
    hat, inverse = norm_stats(x0[...])
    dvec[:, 0:1] += lane_sum(back * hat)
    dvec[:, 1:2] += lane_sum(back)
    dvec[0:1, 2:3] += lane_sum(meta[4:5, :])
    x0_grad = dx1[...] + norm_back(back, hat, inverse, vec[:, 0:1])
    onehot = (rows_of(VPAD, width) == meta[0:1, :].astype(jnp.int32)).astype(f32).astype(bf16)
    for piece in split3(x0_grad):
        dtable[...] += dot(onehot, piece.astype(bf16), NT)

    if last:

        @pl.when(step == pl.num_programs(0) - 1)
        def _():
            columns = dvec[...].T[0:8, :]
            tail[:, 0:model] = dtable[0:TAIL, :]
            tail[0 : VOCAB_ROWS - TAIL, model : 2 * model] = dtable[TAIL:VOCAB_ROWS, :]
            tail[VOCAB_ROWS - TAIL :, model : 2 * model] = jnp.where(rows_of(8, model) < 2, columns, 0.0)
            lane = lax.broadcasted_iota(jnp.int32, (TAIL, 128), 1)
            first = rows_of(TAIL, 128) == 0
            numbers = jnp.where(lane == 0, loss[0:1, 0:1], jnp.where(lane == 1, columns[2:3, 0:1], 0.0))
            tail[:, 2 * model :] = jnp.where(first, numbers, 0.0)


def encode(tail):
    wide = tail.shape[1] - 128
    row = rows_of(tail.shape[0], 128)
    high, middle, rest = split3(tail[0:1, wide:])
    scalars = jnp.where(row == 0, high, jnp.where(row == 1, middle, jnp.where(row == 2, rest, 0.0)))
    return jnp.concatenate([tail[:, :wide], scalars], axis=1)


def decode(tail):
    wide = tail.shape[1] - 128
    row = rows_of(tail.shape[0], 128)
    total = tail[0:1, wide:] + tail[1:2, wide:] + tail[2:3, wide:]
    return jnp.concatenate([tail[:, :wide], jnp.where(row == 0, total, 0.0)], axis=1)


def pack_kernel(swapped, pair, tail, out, keep, send, *, pieces):
    owned = pair.shape[0] - 2 * keep.shape[0]
    shares = swapped[...].astype(f32)
    rows = shares.shape[0] // pieces
    total = None
    for at in range(pieces):
        share = shares[at * rows : (at + 1) * rows, :]
        total = share if total is None else total + share
    both = pair[...].astype(f32)
    half = keep.shape[0]
    first, second = both[0:half, :], both[half : 2 * half, :]
    square = jnp.sum(lane_sum(first * first + second * second), axis=0, keepdims=True)
    is_first = lax.axis_index("core") == 0
    keep[...] = jnp.where(is_first, first, second).astype(bf16)
    send[...] = jnp.where(is_first, second, first).astype(bf16)
    values = tail[...]
    wide = values.shape[1] - 128
    at_square = (rows_of(values.shape[0], 128) == 0) & (lax.broadcasted_iota(jnp.int32, (values.shape[0], 128), 1) == 2)
    values = jnp.concatenate([values[:, :wide], values[:, wide:] + jnp.where(at_square, square, 0.0)], axis=1)
    mine = jnp.concatenate([total, both[2 * half : 2 * half + owned, :]], axis=1)
    out[...] = jnp.concatenate([mine, encode(values)], axis=0).astype(bf16)


def stage_kernel(own, one, two, three, out, *, axis):
    index = lax.axis_index(axis)
    odd, high = lax.rem(index, 2) == 1, index >= 2
    values = [ref[...].astype(f32) for ref in (own, one, two, three)]
    rows = values[0].shape[0] - TAIL
    parts = [value[0:rows, :] for value in values]
    near = jnp.where(odd, parts[1], parts[0]), jnp.where(odd, parts[0], parts[1])
    far = jnp.where(odd, parts[3], parts[2]), jnp.where(odd, parts[2], parts[3])
    placed = [jnp.where(high, far[i], near[i]) for i in range(2)] + [jnp.where(high, near[i], far[i]) for i in range(2)]
    tails = [decode(value[rows:, :]) for value in values]
    total = (tails[0] + tails[1]) + (tails[2] + tails[3])
    out[...] = jnp.concatenate([*placed, encode(total)], axis=0).astype(bf16)


def adam_step(weight, grad, drift, spread, rate):
    drift = FIRST_DECAY * drift + (1.0 - FIRST_DECAY) * grad
    spread = SECOND_DECAY * spread + (1.0 - SECOND_DECAY) * grad * grad
    adjusted = (
        drift
        / (1.0 - FIRST_DECAY**STEP)
        / (jnp.sqrt(spread / (1.0 - SECOND_DECAY**STEP)) + ADAM_EPS)
    )
    return (weight - rate * (adjusted + WEIGHT_DECAY * weight), drift, spread)


def update_kernel(*refs, groups, early_groups):
    early_mine, early_other, last_mine, last_other, pair_keep, pair_sent = refs[:6]
    ins, outs = refs[6:21], refs[21:41]
    pair_out, norm_out, g_in, g_out, g_table, g_vec, scale, sems = refs[41:49]
    held = refs[49:]
    step = pl.program_id(0)
    steps = g_in.shape[0] // outs[4].shape[0]

    def copy(array, chunk):
        span = pl.ds(chunk * outs[4].shape[0], outs[4].shape[0])
        return pltpu.make_async_copy(ins[3 + array].at[span], held[array].at[span], sems.at[array, chunk])

    @pl.when(step == 0)
    def _():
        for chunk in range(steps):
            for array in range(6):
                copy(array, chunk).start()

    vocab, model = ins[0].shape
    half_rows = early_mine.shape[0]
    piece = model // groups
    last_width = 3 * piece * (groups - early_groups)
    after = model - half_rows

    @pl.when(step == 0)
    def _():
        is_first = lax.axis_index("core") == 0

        def halves(mine, other):
            mine, other = mine[0:half_rows, :].astype(f32), other[0:half_rows, :].astype(f32)
            return jnp.where(is_first, mine, other), jnp.where(is_first, other, mine)

        squares = jnp.zeros((1, 128), f32)

        def add_squares(values):
            rows = jnp.sum(values * values, axis=0, keepdims=True)
            total = None
            for at in range(0, rows.shape[1], 128):
                total = rows[:, at : at + 128] if total is None else total + rows[:, at : at + 128]
            return total

        for mine, other, first, size in (
            (early_mine, early_other, 0, early_groups),
            (last_mine, last_other, early_groups, groups - early_groups),
        ):
            upper, lower = halves(mine, other)
            rest_upper, rest_lower = upper[:, last_width:], lower[:, last_width:]
            upper, lower = upper[:, : 3 * piece * size], lower[:, : 3 * piece * size]
            squares += add_squares(upper) + add_squares(lower)
            for group in range(size):
                for part in range(3):
                    source = slice((group * 3 + part) * piece, (group * 3 + part + 1) * piece)
                    at = part * model + (first + group) * piece
                    g_in[0:half_rows, at : at + piece] = upper[:, source]
                    g_in[half_rows:model, at : at + piece] = lower[0:after, source]
                    into = slice((first + group) * piece, (first + group + 1) * piece)
                    g_vec[2 + part : 3 + part, into] = lower[after : after + 1, source]
        upper, lower = rest_upper, rest_lower
        g_out[0:half_rows, :] = upper
        g_out[half_rows:, :] = lower[0:after, :]
        others = lower[after : after + REST_TABLE, :]
        g_vec[5:15, :] = others[0:10, :]
        tails = [decode(ref[half_rows:, :].astype(f32)) for ref in (last_mine, last_other)]
        final = tails[0] + tails[1]
        scalars = final[:, 2 * model :]
        late = jnp.concatenate([final[:, 0:model], final[0 : VOCAB_ROWS - TAIL, model : 2 * model]], axis=0)
        table = late + lower[after + REST_TABLE : after + REST_TABLE + VOCAB_ROWS, :]
        g_table[...] = table
        tail = final[VOCAB_ROWS - TAIL :, model : 2 * model]
        g_vec[0:2, :] = tail[0:2, :]
        squares += add_squares(upper) + add_squares(lower[0:after, :]) + add_squares(others) + add_squares(table)
        squares += add_squares(tail[0:2, :])
        total = lane_sum(squares) + scalars[0:1, 2:3]
        crops = scalars[0:1, 1:2]
        norm = jnp.sqrt(total) / crops
        scale[...] = jnp.broadcast_to(jnp.minimum(1.0, CLIP_NORM / (norm + 1e-06)) / crops, scale.shape)
        pair_out[0] = jnp.sum(scalars[0:1, 0:1])
        pair_out[1] = jnp.sum(crops)
        norm_out[0] = jnp.sum(norm)

    factor = scale[0:1, 0:1]

    def update(which, grad, rate, span=...):
        source = held[which * 3 - 3 : which * 3] if span is not ... else ins[which * 3 : which * 3 + 3]
        weight, drift, spread = (ref[span] for ref in source)
        fresh, drift, spread = adam_step(weight, grad * factor, drift, spread, rate)
        out = outs[which * 4 : which * 4 + 4]
        out[0][...] = fresh
        out[1][...] = drift
        out[2][...] = spread
        out[3][...] = fresh.astype(bf16)

    @pl.when(step == 0)
    def _():
        update(0, g_table[0:vocab, :], 0.05)
        keep, sent = pair_keep[...].astype(f32), pair_sent[...].astype(f32)
        is_first = lax.axis_index("core") == 0
        update(3, jnp.stack([jnp.where(is_first, keep, sent), jnp.where(is_first, sent, keep)]), 0.05)
        update(4, g_vec[0:15, :], 0.2)

    for array in range(6):
        copy(array, step).wait()
    rows = outs[4].shape[0]
    span = pl.ds(pl.multiple_of(step * rows, rows), rows)
    update(1, g_in[span, :], 0.05, span)
    update(2, g_out[span, :], 0.1, span)


def whole(shape):
    return pl.BlockSpec(shape, lambda *_: (0,) * len(shape), pipeline_mode=pl.Buffered(1))


def shaped(shape, dtype):
    return jax.ShapeDtypeStruct(shape, dtype)


def limits(mib):
    return pltpu.CompilerParams(vmem_limit_bytes=mib * MIB)


def cost(flops, moved, transcendentals=0):
    return pl.CostEstimate(flops=int(flops), bytes_accessed=int(moved), transcendentals=int(transcendentals))


def rotary_constants(rows):
    freq = np.float32(10000.0) ** (-np.arange(0, HEAD_DIM, 2, dtype=np.float32) / np.float32(HEAD_DIM))
    angle = np.arange(rows, dtype=np.float32)[None, :] * freq[:, None].astype(np.float32)
    return np.cos(angle).astype(np.float32), np.sin(angle).astype(np.float32)


def body(
    columns,
    deep,
    true_ids,
    picked,
    replace_kinds,
    random_ids,
    splits,
    embedding,
    projection,
    outward,
    feedforward,
    vectors,
    embedding_drift,
    embedding_spread,
    projection_drift,
    projection_spread,
    outward_drift,
    outward_spread,
    feedforward_drift,
    feedforward_spread,
    vectors_drift,
    vectors_spread,
):
    tokens = true_ids.shape[0]
    slots = splits.shape[0]
    rows = tokens // slots
    half = rows // 2
    vocab, model = embedding.shape
    heads = model // HEAD_DIM
    bias_rows = chunks_of_bias(model)
    block = half
    blocks = tokens // block
    wide = FF // columns
    devices = columns * deep * 2
    chips = ("col", "deep")
    everywhere = ("col", "deep", "core")

    pair_all = lax.all_gather(feedforward.astype(bf16), everywhere, axis=1, tiled=True)
    pair_all = pair_all.reshape(2, columns, model, wide)

    masked = (picked == 1) & (replace_kinds < 8)
    swapped = (picked == 1) & (replace_kinds == 8)
    input_ids = jnp.where(masked, MASK_ID, jnp.where(swapped, random_ids, true_ids))
    within = jnp.arange(rows, dtype=jnp.int32)
    second = ((within[None, :] >= half).astype(jnp.int32) * splits[:, None]).astype(f32)
    pick = picked.astype(f32).reshape(slots, rows)
    half_counts = jnp.sum(pick.reshape(slots, 2, half), axis=2)
    split = splits[:, None].astype(f32)
    half_counts = jnp.where(split > 0.5, half_counts, jnp.sum(half_counts, axis=1, keepdims=True))
    token_weight = (pick.reshape(slots, 2, half) / half_counts[:, :, None]).reshape(tokens)
    zero = jnp.zeros((tokens,), f32)
    crop_share = jnp.broadcast_to((1 + splits).astype(f32)[:, None] * (1.0 / rows), (slots, rows)).reshape(tokens)
    meta = jnp.stack(
        [input_ids.astype(f32), true_ids.astype(f32), second.reshape(-1), token_weight, crop_share, zero, zero, zero]
    )
    cos_np, sin_np = rotary_constants(rows)
    cos_table, sin_table = jnp.asarray(cos_np), jnp.asarray(sin_np)
    twice_cos, twice_sin = (jnp.asarray(np.tile(t[:, :half], (1, 2))) for t in (cos_np, sin_np))

    def by_block(count):
        return pl.BlockSpec((count, block), lambda i: (0, i))

    def heads_block(count):
        return pl.BlockSpec((heads, count, block), lambda i: (0, 0, i))

    first_half = pl.BlockSpec((HALF, block), lambda i: (0, 0))
    own_half = pl.BlockSpec((HALF, block), lambda i: (0, i % 2))
    x0, normed, q_ext, k_ext, v_ext = pl.pallas_call(
        qkv_kernel,
        grid=(blocks,),
        in_specs=[by_block(8), whole((vocab, model)), whole((model, 3 * model)), whole(vectors.shape),
                  first_half, own_half, first_half, own_half],
        out_specs=[by_block(model), by_block(model + 16), heads_block(EXT), heads_block(EXT), heads_block(EXT)],
        out_shape=[shaped((model, tokens), f32), shaped((model + 16, tokens), bf16)]
        + [shaped((heads, EXT, tokens), bf16)] * 3,
        scratch_shapes=[pltpu.VMEM((model, 128), bf16), pltpu.VMEM((3 * model, model), bf16), pltpu.VMEM((model, 128), f32),
                        pltpu.VMEM((128, model), f32)],
        compiler_params=limits(56),
        cost_estimate=cost(2 * 3 * model * model * tokens, 20 * model * tokens),
        name="embed_and_qkv",
    )(meta, embedding, projection, vectors, cos_table, cos_table, sin_table, sin_table)

    per = 4

    def head_group(count, size, first=0):
        return pl.BlockSpec((size, count, rows), lambda s, g: (first + g, 0, s))

    attended, q_next = pl.pallas_call(
        attention_kernel,
        grid=(slots, heads // per),
        in_specs=[head_group(EXT, per)] * 3,
        out_specs=[head_group(HEAD_DIM, per), head_group(EXT, per)],
        out_shape=[shaped((heads, HEAD_DIM, tokens), bf16), shaped((heads, EXT, tokens), bf16)],
        compiler_params=limits(56),
        cost_estimate=cost(2 * 16 * model * rows * tokens, 12 * model * tokens, heads * rows * tokens),
        name="attention",
    )(q_ext, k_ext, v_ext)
    attended = attended.reshape(model, tokens)

    half_rows = (model + 128) // 2
    owned = -(-half_rows // (8 * columns * deep)) * 8
    dx1, do_ext, keep_pair, send_pair, keep_rest, send_rest, loss = pl.pallas_call(
        middle_kernel,
        grid=(blocks,),
        in_specs=[by_block(8), by_block(model), by_block(model), whole((model, model)),
                  pl.BlockSpec(memory_space=pl.ANY), whole((vocab, model)), whole(vectors.shape)],
        out_specs=[by_block(model), heads_block(EXT), pl.BlockSpec(memory_space=pl.ANY), pl.BlockSpec(memory_space=pl.ANY),
                   whole((half_rows, model)), whole((half_rows, model)), whole((8, 128))],
        out_shape=[shaped((model, tokens), f32), shaped((heads, EXT, tokens), bf16), shaped((columns * model, wide), bf16),
                   shaped((columns * model, wide), bf16), shaped((half_rows, model), bf16), shaped((half_rows, model), bf16),
                   shaped((8, 128), f32)],
        scratch_shapes=[pltpu.VMEM((model, FF), bf16), pltpu.VMEM((model, FF), bf16), pltpu.VMEM((FF, model), bf16),
                        pltpu.VMEM((FF, model), bf16), pltpu.VMEM((FF, block), bf16), pltpu.VMEM((FF, block), bf16),
                        pltpu.VMEM((model, FF), f32), pltpu.VMEM((model, FF), f32),
                        pltpu.VMEM((model + 128, model), f32), pltpu.VMEM((VPAD, model), f32), pltpu.VMEM((model, 128), f32),
                        pltpu.VMEM((model, 128), f32), pltpu.VMEM((128, model), f32),
                        pltpu.VMEM((VPAD, model), bf16), pltpu.VMEM((model, 128), bf16),
                        pltpu.VMEM((model, model), bf16), pltpu.VMEM((model, model), bf16), pltpu.SemaphoreType.DMA((2 + 2 * columns,))],
        compiler_params=limits(62),
        cost_estimate=cost(2 * tokens * model * (6 * FF + 3 * model), 14 * model * tokens + 16 * model * FF, FF * tokens),
        name="feedforward_and_head",
    )(meta, x0, attended, outward, pair_all, embedding, vectors)

    count = columns * deep

    def swap(values, axes):
        return lax.all_to_all(values, axes, 0, 0, tiled=True)

    def over_core(values):
        return lax.ppermute(values, "core", [(0, 1), (1, 0)])

    def add_up(values, pieces):
        return jnp.sum(values.reshape((pieces, -1) + values.shape[1:]).astype(f32), axis=0)

    def pair_sum(keep, sent):
        return (keep.astype(f32) + sent.astype(f32)).astype(bf16)

    def pad_rows(values):
        return jnp.pad(values, ((0, owned * count - half_rows), (0, 0)))

    def to_owner(values):
        return swap(pad_rows(values), chips)

    def gather4(values, axis):
        one, two, three = (lax.ppermute(values, axis, [(i, i ^ d) for i in range(4)]) for d in (1, 2, 3))
        index = lax.axis_index(axis)
        odd, high = index % 2 == 1, index >= 2
        near = jnp.where(odd, one, values), jnp.where(odd, values, one)
        far = jnp.where(odd, three, two), jnp.where(odd, two, three)
        return jnp.concatenate(
            [jnp.where(high, far[i], near[i]) for i in range(2)] + [jnp.where(high, near[i], far[i]) for i in range(2)],
            axis=0,
        )

    def gather_deep(values):
        return gather4(values, "deep") if deep == 4 else lax.all_gather(values, "deep", axis=0, tiled=True)

    def gather_col(values):
        return (gather4(values, "col") if columns == 4 else lax.all_gather(values, "col", axis=0, tiled=True))[:half_rows]

    def together(first, *others):
        return lax.optimization_barrier((first, *others))

    pair_sent, rest_sent = over_core(send_pair), over_core(send_rest)
    per_call = 4
    width = 3 * per_call * HEAD_DIM
    grads = None
    keeps, sents = [], []
    groups = heads // per_call
    for first in range(groups):
        chained = grads is not None

        def group(count, first=first):
            return pl.BlockSpec((per_call, count, rows), lambda s: (first, 0, s))

        table_spec = pl.BlockSpec((HALF, rows), lambda s: (0, 0))
        outs = pl.pallas_call(
            functools.partial(attention_back_kernel, chunk=half, chained=chained),
            grid=(slots,),
            in_specs=[group(EXT)] * 4
            + [pl.BlockSpec((model + 16, rows), lambda s: (0, s)), pl.BlockSpec((8, rows), lambda s: (0, s))]
            + [table_spec] * 4
            + [pl.BlockSpec(memory_space=pl.ANY)] * (3 if chained else 0),
            out_specs=[group(HEAD_DIM)] * 3 + [pl.BlockSpec((half_rows, width), lambda s: (0, 0))] * 2,
            out_shape=[shaped((heads, HEAD_DIM, tokens), bf16)] * 3 + [shaped((half_rows, width), bf16)] * 2,
            scratch_shapes=[pltpu.VMEM((width, rows), bf16), pltpu.VMEM((2 * half_rows, width), f32)],
            input_output_aliases={10: 0, 11: 1, 12: 2} if chained else {},
            compiler_params=limits(56),
            cost_estimate=cost(2 * 40 * width // 3 * rows * tokens, 20 * width * tokens, per_call * rows * tokens),
            name="attention_back",
        )(q_next, k_ext, v_ext, do_ext, normed, meta, twice_cos, cos_table, twice_sin, sin_table, *(grads or ()))
        grads = outs[:3]
        keeps.append(outs[3])
        sents.append(over_core(outs[4]))
        if first == 0:
            pair = pair_sum(keep_pair.reshape(count, -1, wide), pair_sent.reshape(count, -1, wide))
            rest_half = pad_rows(pair_sum(keep_rest, rest_sent)).reshape(count, owned, model)
            pair = jnp.concatenate([pair, rest_half], axis=1).reshape(-1, wide)
            do_ext, pair = together(do_ext, pair)
            pair = lax.psum_scatter(pair, chips, scatter_dimension=0, tiled=True)
        elif first == groups - 2:
            early = jnp.concatenate([pair_sum(keeps[i], sents[i]) for i in range(groups - 2)], axis=1)
            do_ext, early = together(do_ext, early)
            early = to_owner(early)
        elif first == groups - 1:
            late_half = jnp.concatenate([pair_sum(keeps[i], sents[i]) for i in range(groups - 2, groups)], axis=1)
            early = add_up(early, count).astype(bf16)
            dx1, late_half, early = together(dx1, late_half, early)
            late_half = to_owner(late_half)
            early = gather_deep(early)
    dq, dk, dv = (grad.reshape(model, tokens) for grad in grads)

    back_out = [shaped((model, 128), f32), shaped((VPAD, model), f32)]
    back_room = [pltpu.VMEM((model, 3 * model), bf16), pltpu.VMEM((model, 128), f32), pltpu.VMEM((128, model), f32)]

    def input_back(part, extra):
        def by_part(rows_):
            return pl.BlockSpec((rows_, block), lambda i: (0, i + part * (blocks // 2)))

        last = part == 1
        room = [pltpu.VMEM(shape.shape, f32) for shape in back_out]
        return pl.pallas_call(
            functools.partial(input_back_kernel, last=last),
            grid=(blocks // 2,),
            in_specs=[by_part(8)] + [by_part(model)] * 5 + [whole((model, 3 * model)), whole(vectors.shape)]
            + [whole(array.shape) for array in extra],
            out_specs=[whole((TAIL, 2 * model + 128))] if last else [whole(shape.shape) for shape in back_out],
            out_shape=[shaped((TAIL, 2 * model + 128), f32)] if last else back_out,
            scratch_shapes=back_room + (room if last else []),
            compiler_params=limits(56),
            cost_estimate=cost(3 * model * model * tokens, 10 * model * tokens),
            name="input_back",
        )(meta, x0, dq, dk, dv, dx1, projection, vectors, *extra)

    halfway = input_back(0, ())
    dvec_half, dtable_half, early = together(*halfway, early)
    early = gather_col(early)
    (tail,) = input_back(1, (loss, dvec_half, dtable_half))
    tail, pair, early, late_half = together(tail, pair, early, late_half)
    early_other = over_core(early)

    def call_small(kernel, args, outs, name):
        return pl.pallas_call(
            kernel,
            in_specs=[pl.BlockSpec(memory_space=pltpu.VMEM)] * len(args),
            out_specs=[pl.BlockSpec(memory_space=pltpu.VMEM)] * len(outs),
            out_shape=[shaped(shape, bf16) for shape in outs],
            compiler_params=limits(40),
            cost_estimate=cost(1e6, 4e6),
            name=name,
        )(*args)

    own = (pair.shape[0] - owned) // 2
    last_width = late_half.shape[1] + model
    if columns == 4 and deep == 4 and owned == TAIL and last_width == tail.shape[1]:
        packed, pair_keep, pair_sent = call_small(
            functools.partial(pack_kernel, pieces=count), (late_half, pair, tail),
            [(owned + TAIL, last_width), (own, wide), (own, wide)], "pack",
        )
        pair_sent = over_core(pair_sent)
        for axis in ("deep", "col"):
            got = [lax.ppermute(packed, axis, [(i, i ^ d) for i in range(4)]) for d in (1, 2, 3)]
            merged = 4 * (packed.shape[0] - TAIL) + TAIL
            (packed,) = call_small(functools.partial(stage_kernel, axis=axis), (packed, *got), [(merged, last_width)], "stage")
    else:
        is_first = lax.axis_index("core") == 0
        pair_keep = jnp.where(is_first, pair[:own], pair[own : 2 * own])
        pair_sent = over_core(jnp.where(is_first, pair[own : 2 * own], pair[:own]))
        square = jnp.sum(jnp.square(pair[: 2 * own].astype(f32)))
        tail = lax.psum(tail.at[0, 2 * model + 2].add(square), chips)
        scalars = tail[0:1, 2 * model :]
        high = lax.reduce_precision(scalars, 8, 7)
        middle = lax.reduce_precision(scalars - high, 8, 7)
        numbers = jnp.concatenate([high, middle, scalars - high - middle, jnp.zeros((TAIL - 3, 128), f32)], axis=0)
        tail = jnp.pad(jnp.concatenate([tail[:, : 2 * model], numbers], axis=1), ((0, 0), (0, last_width - tail.shape[1])))
        packed = jnp.concatenate([add_up(late_half, count).astype(bf16), pair[2 * own :]], axis=1)
        packed = jnp.concatenate([gather_col(gather_deep(packed)), tail.astype(bf16)], axis=0)
    packed_other = over_core(packed)

    steps = 10
    state = (
        (embedding, embedding_drift, embedding_spread),
        (projection, projection_drift, projection_spread),
        (outward, outward_drift, outward_spread),
        (feedforward, feedforward_drift, feedforward_spread),
        (vectors, vectors_drift, vectors_spread),
    )

    def state_spec(array):
        if array.shape[0] == model:
            return pl.BlockSpec((model // steps, array.shape[1]), lambda i: (i, 0))
        return whole(array.shape)

    grads_in = (early, early_other, packed, packed_other, pair_keep, pair_sent)
    results = pl.pallas_call(
        functools.partial(update_kernel, groups=groups, early_groups=groups - 2),
        grid=(steps,),
        in_specs=[whole(array.shape) for array in grads_in] + [
            pl.BlockSpec(memory_space=pl.ANY) if array.shape[0] == model else whole(array.shape) for three in state for array in three
        ],
        out_specs=[state_spec(three[0]) for three in state for _ in range(4)]
        + [pl.BlockSpec(memory_space=pltpu.SMEM)] * 2,
        out_shape=[shaped(three[0].shape, dtype) for three in state for dtype in (f32, f32, f32, bf16)]
        + [shaped((2,), f32), shaped((1,), f32)],
        scratch_shapes=[pltpu.VMEM((model, 3 * model), f32), pltpu.VMEM((model, model), f32), pltpu.VMEM((VOCAB_ROWS, model), f32),
                        pltpu.VMEM((16, model), f32), pltpu.VMEM((8, 128), f32), pltpu.SemaphoreType.DMA((6, steps))]
        + [pltpu.VMEM(array.shape, f32) for three in state[1:3] for array in three],
        compiler_params=limits(56),
        cost_estimate=cost(60 * 4 * model * model, 4 * 30 * model * model),
        name="clip_and_adamw",
    )(*grads_in, *(array for three in state for array in three))
    return (results[20], results[21].reshape(()), *results[:20])


def solution(mesh):
    columns, row = mesh.shape["col"], mesh.shape["row"]
    fine = jax.sharding.Mesh(mesh.devices.reshape(columns, row // 2, 2), ("col", "deep", "core"))
    split_all, tiles, full = P(("col", "deep", "core")), P(None, ("deep", "core"), "col"), P()
    return jax.shard_map(
        functools.partial(body, columns, row // 2),
        mesh=fine,
        in_specs=(split_all,) * 5 + (full,) * 3 + (tiles,) + (full,) * 7 + (tiles,) * 2 + (full,) * 2,
        out_specs=(full,) * 14 + (tiles,) * 4 + (full,) * 4,
        check_vma=False,
    )
```

```python
import functools
import math

import jax
import jax.numpy as jnp
import numpy as np
from jax import lax
from jax.experimental import pallas as pl
from jax.experimental.pallas import tpu as pltpu
from jax.sharding import PartitionSpec as P

HEAD_DIM = 32
HALF = HEAD_DIM // 2
EXT = HEAD_DIM + 16
FF = 2560
STEP = 10
VPAD = 48
VOCAB_ROWS = 40
TAIL = 48
UNITS = 640
THIRD = 40

EPS_NORM = 1e-05
CLIP_NORM = 0.002
FIRST_DECAY = 0.5
SECOND_DECAY = 0.5
ADAM_EPS = 1e-08
WEIGHT_DECAY = 0.01
MASK_ID = 32
MASKED = 1e30
SAFE_EXPONENT = 40.0

LOG2E = math.log2(math.e)
SCALE = HEAD_DIM ** (-0.5)
MIB = 2**20

bf16 = jnp.bfloat16
f32 = jnp.float32

NN = ((1,), (0,))
NT = ((1,), (1,))
TN = ((0,), (0,))


def dot(left, right, dims=NN):
    return lax.dot_general(left, right, (dims, ((), ())), preferred_element_type=f32)


def split3(values):
    high = values.astype(bf16).astype(f32)
    rest = values - high
    middle = rest.astype(bf16).astype(f32)
    return high, middle, rest - middle


def norm_stats(values):
    center = values - jnp.mean(values, axis=0, keepdims=True)
    inverse = lax.rsqrt(jnp.mean(center * center, axis=0, keepdims=True) + EPS_NORM)
    return center * inverse, inverse


def norm_back(grad, hat, inverse, gain):
    scaled = grad * gain
    return inverse * (
        scaled
        - jnp.mean(scaled, axis=0, keepdims=True)
        - hat * jnp.mean(scaled * hat, axis=0, keepdims=True)
    )


def rows_of(count, width):
    return lax.broadcasted_iota(jnp.int32, (count, width), 0)


def split_halves(total, keep, send):
    rows = keep.shape[0]
    first, second = total[0:rows, :], total[rows:, :]
    is_first = lax.axis_index("core") == 0
    keep[...] = jnp.where(is_first, first, second).astype(bf16)
    send[...] = jnp.where(is_first, second, first).astype(bf16)


def lane_sum(values):
    return jnp.sum(values, axis=1, keepdims=True)


def columns_of(vectors, wide):
    wide[...] = jnp.zeros_like(wide)
    wide[0 : vectors.shape[0], :] = vectors[...]
    return wide[...].T


def qkv_kernel(
    true_ids, picked, kinds, random_ids, slot_picked, splits, embedding, projection, vectors, cos_a, cos_b, sin_a, sin_b,
    meta, x0, low, q_ext, k_ext, v_ext, rounded,
    table, weight, vec, wide,
):
    width = true_ids.shape[1]
    heads = q_ext.shape[0]
    model = x0.shape[0]
    vocab = embedding.shape[0]
    block = pl.program_id(0)

    @pl.when(pl.program_id(0) == 0)
    def _():
        vec[...] = columns_of(vectors, wide)
        wide[...] = jnp.zeros_like(wide)
        for part, piece in enumerate(split3(embedding[...])):
            wide[part * THIRD : part * THIRD + vocab, :] = piece
        table[...] = wide[...].T.astype(bf16)
        for part in range(3):
            span = slice(part * model, (part + 1) * model)
            rounded[:, span] = projection[:, span].astype(bf16)
            weight[span, :] = rounded[:, span].T

    is_pick = picked[...] == 1
    masked, swapped = is_pick & (kinds[...] < 8), is_pick & (kinds[...] == 8)
    ids = jnp.where(masked, MASK_ID, jnp.where(swapped, random_ids[...], true_ids[...]))
    split = splits[block // 2]
    second = jnp.full((1, width), split * (block % 2), jnp.int32).astype(f32)
    picks = picked[...].astype(f32)
    counts = lane_sum(jnp.where(split > 0, picks, 0.0))
    counts += lane_sum(jnp.where(split > 0, 0.0, slot_picked[...].astype(f32)))
    crop_share = jnp.full((1, width), 1 + split, jnp.int32).astype(f32) * (1.0 / slot_picked.shape[1])
    at = rows_of(8, width)
    rows = jnp.where(at == 0, ids.astype(f32), jnp.where(at == 1, true_ids[...].astype(f32), jnp.where(at == 2, second, 0.0)))
    meta[...] = jnp.where(at == 3, picks / counts, jnp.where(at == 4, crop_share, rows))
    vocab3 = rows_of(128, width)
    onehot = ((vocab3 == ids) | (vocab3 == ids + THIRD) | (vocab3 == ids + 2 * THIRD)).astype(f32).astype(bf16)
    embedded = dot(table[...], onehot)
    x0[...] = embedded
    hat, _ = norm_stats(embedded)
    normed = (hat * vec[:, 0:1] + vec[:, 1:2]).astype(bf16)
    row = rows_of(EXT - HEAD_DIM, width)
    low[0:model, :] = normed
    low[model : model + 16, :] = jnp.where(row == 0, 1.0, 0.0).astype(bf16)
    in_second = second > 0.5
    cos = jnp.where(in_second, cos_a[...], cos_b[...])
    sin = jnp.where(in_second, sin_a[...], sin_b[...])
    q_rows = jnp.where(row == 0, second, jnp.where(row == 1, 1.0 - second, 0.0)).astype(bf16)
    k_rows = jnp.where(
        row == 0,
        -MASKED * (1.0 - second),
        jnp.where(row == 1, -MASKED * second, jnp.where(row < 5, 1.0, 0.0)),
    ).astype(bf16)
    v_rows = jnp.where(row < 3, 1.0, 0.0).astype(bf16)
    for part, out, extra in ((0, q_ext, q_rows), (1, k_ext, k_rows), (2, v_ext, v_rows)):
        base = part * model
        mixed = dot(weight[base : base + model, :], normed) + vec[:, 2 + part : 3 + part]
        for head in range(heads):
            one = mixed[head * HEAD_DIM : head * HEAD_DIM + HALF, :]
            two = mixed[head * HEAD_DIM + HALF : (head + 1) * HEAD_DIM, :]
            if part < 2:
                one, two = one * cos - two * sin, two * cos + one * sin
            out[head, 0:HALF, :] = one.astype(bf16)
            out[head, HALF:HEAD_DIM, :] = two.astype(bf16)
            out[head, HEAD_DIM:EXT, :] = extra


def attention_kernel(q_ext, k_ext, v_ext, out, raised, inverse):
    heads, _, width = q_ext.shape
    factor = LOG2E * SCALE

    def longest(array):
        values = array[:, 0:HEAD_DIM, :].astype(f32)
        return jnp.max(jnp.sum(values * values, axis=1))

    def finish(head):
        mixed = dot(v_ext[head], raised[head], NT)
        share = 1.0 / mixed[HEAD_DIM : HEAD_DIM + 1, :]
        out[head] = (mixed[0:HEAD_DIM, :] * share).astype(bf16)
        inverse[head] = jnp.broadcast_to(share, (8, width))

    small = longest(q_ext) * longest(k_ext) * factor**2 <= SAFE_EXPONENT**2

    @pl.when(small)
    def _():
        for head in range(heads):
            raised[head] = jnp.exp2(dot(q_ext[head], k_ext[head], TN) * factor).astype(bf16)
            finish(head)

    @pl.when(jnp.logical_not(small))
    def _():
        for head in range(heads):
            scores = dot(q_ext[head], k_ext[head], TN)
            top = jnp.max(scores, axis=1, keepdims=True)
            raised[head] = jnp.exp2((scores - top) * factor).astype(bf16)
            finish(head)


def attention_back_kernel(
    q_ext, k_ext, v_ext, do_ext, raised, low, meta, cos_a, cos_b, sin_a, sin_b, *rest,
    chunk, chained, carried, finished, first_head, from_slot,
):
    rest = list(rest[3:] if chained else rest)
    before = rest.pop(0) if carried else None
    dq, dk, dv = rest[:3]
    if finished:
        keep, send, grads, held, sems, total = rest[3:]
    else:
        total, grads, held, sems = rest[3:]
    slot = pl.program_id(0)
    heads, _, width = q_ext.shape

    def fetch(which, head):
        source = raised.at[first_head + head, pl.ds((from_slot + which) * width, width)]
        return pltpu.make_async_copy(source, held.at[which * heads + head], sems.at[which * heads + head])

    @pl.when(slot == 0)
    def _():
        for which in range(held.shape[0] // heads):
            for head in range(heads):
                fetch(which, head).start()

    in_second = meta[2:3, :] > 0.5
    cos = jnp.where(in_second, cos_a[...], cos_b[...])
    sin = jnp.where(in_second, sin_a[...], sin_b[...])
    for head in range(heads):
        fetch(slot, head).wait()
        keys = k_ext[head]
        q_parts = []
        k_total = v_total = None
        for at in range(0, width, chunk):
            piece = slice(at, at + chunk)
            queries, outs = q_ext[head, :, piece], do_ext[head, :, piece]
            prob = held[slot * heads + head, piece, :]
            inner = dot(outs, v_ext[head], TN)
            score_grad = (prob.astype(f32) * inner).astype(bf16)
            q_parts.append(dot(keys[0:HEAD_DIM, :], score_grad, NT))
            k_part = dot(queries[0:HEAD_DIM, :], score_grad)
            v_part = dot(outs[0:HEAD_DIM, :], prob)
            k_total = k_part if k_total is None else k_total + k_part
            v_total = v_part if v_total is None else v_total + v_part
        for part, (out, grad) in enumerate(((dq, jnp.concatenate(q_parts, axis=1)), (dk, k_total), (dv, v_total))):
            one, two = grad[0:HALF, :], grad[HALF:HEAD_DIM, :]
            if part < 2:
                one, two = one * SCALE, two * SCALE
                one, two = one * cos + two * sin, two * cos - one * sin
            out[head, 0:HALF, :] = one.astype(bf16)
            out[head, HALF:HEAD_DIM, :] = two.astype(bf16)
            base = (part * heads + head) * HEAD_DIM
            grads[base : base + HEAD_DIM, :] = out[head]
    share = dot(low[...], grads[...], NT)
    rows = share.shape[0]

    @pl.when(slot == 0)
    def _():
        total[0:rows, :] = before[0:rows, :] + share if carried else share

    @pl.when(slot > 0)
    def _():
        total[0:rows, :] += share

    if finished:

        @pl.when(slot == pl.num_programs(0) - 1)
        def _():
            total[rows:, :] = jnp.zeros((total.shape[0] - rows, total.shape[1]), f32)
            split_halves(total, keep, send)


def middle_kernel(
    meta, x0, attended, inverse, outward, pair_all, embedding, vectors,
    dx1, do_ext, keep_pair, send_pair, keep_rest, send_rest, dtable, loss,
    w_up, w_down, up_t, down_t, act, slope, dw_up, dw_down, dw_out, dvec, vec, wide, table, table_t, w_out, w_out_t,
    sems,
):
    step = pl.program_id(0)
    chunks = pair_all.shape[1]
    model, width = x0.shape
    hidden_units = w_up.shape[1]
    unit = hidden_units // chunks
    heads = do_ext.shape[0]
    vocab = embedding.shape[0]

    @pl.when(step == 0)
    def _():
        fetches = []
        for side, into in enumerate((w_up, w_down)):
            for part in range(chunks):
                fetch = pltpu.make_async_copy(
                    pair_all.at[side, part], into.at[:, pl.ds(part * unit, unit)], sems.at[2 + side * chunks + part]
                )
                fetch.start()
                fetches.append(fetch)
        vec[...] = columns_of(vectors, wide)
        wide[...] = jnp.zeros_like(wide)
        wide[0:vocab, :] = embedding[...]
        table[...] = wide[0:VPAD, :].astype(bf16)
        table_t[...] = wide[...].T.astype(bf16)
        w_out[...] = outward[...].astype(bf16)
        w_out_t[...] = w_out[...].T
        dw_up[...] = jnp.zeros_like(dw_up)
        dw_down[...] = jnp.zeros_like(dw_down)
        dw_out[...] = jnp.zeros_like(dw_out)
        dtable[...] = jnp.zeros_like(dtable)
        dvec[...] = jnp.zeros_like(dvec)
        loss[...] = jnp.zeros_like(loss)
        for fetch in fetches:
            fetch.wait()
        for part in range(chunks):
            span = slice(part * unit, (part + 1) * unit)
            up_t[span, :] = w_up[:, span].T
            down_t[span, :] = w_down[:, span].T

    def col(index):
        return vec[:, index : index + 1]

    after = 8 + chunks_of_bias(model)
    x1 = x0[...] + dot(w_out_t[...], attended[...]) + col(5)
    hat_two, inverse_two = norm_stats(x1)
    c_low = (hat_two * col(6) + col(7)).astype(bf16)
    for first in range(0, hidden_units, UNITS):
        inner = dot(up_t[first : first + UNITS, :], c_low)
        for at in range(first, first + UNITS, model):
            hidden = inner[at - first : at - first + model, :] + col(8 + at // model)
            cdf = 0.5 + 0.5 * lax.erf(hidden * (0.5**0.5))
            density = jnp.exp(hidden * hidden * -0.5) * (1.0 / math.sqrt(2.0 * math.pi))
            act[at : at + model, :] = (hidden * cdf).astype(bf16)
            slope[at : at + model, :] = (cdf + hidden * density).astype(bf16)
    x2 = x1 + dot(w_down[...], act[...]) + col(after)
    hat_end, inverse_end = norm_stats(x2)
    f_low = (hat_end * col(after + 1) + col(after + 2)).astype(bf16)
    vocab_rows = rows_of(VPAD, width)
    logits = jnp.where(vocab_rows < vocab, dot(table[...], f_low), -MASKED)
    top = jnp.max(logits, axis=0, keepdims=True)
    raised = jnp.exp(logits - top)
    total = jnp.sum(raised, axis=0, keepdims=True)
    target = (vocab_rows == meta[1:2, :].astype(jnp.int32)).astype(f32)
    chosen = jnp.sum(logits * target, axis=0, keepdims=True)
    weight = meta[3:4, :]
    loss[0:1, :] += jnp.broadcast_to(lane_sum(weight * (jnp.log(total) + top - chosen)), (1, loss.shape[1]))
    logit_grad = (weight * (raised / total - target)).astype(bf16)
    dtable[...] += dot(logit_grad, f_low, NT)
    f_grad = dot(table_t[:, 0:VPAD], logit_grad)
    dvec[:, 4 + chunks : 5 + chunks] += lane_sum(f_grad * hat_end)
    dvec[:, 5 + chunks : 6 + chunks] += lane_sum(f_grad)
    x2_grad = norm_back(f_grad, hat_end, inverse_end, col(after + 1))
    g_low = x2_grad.astype(bf16)
    dvec[:, 3 + chunks : 4 + chunks] += lane_sum(g_low.astype(f32))
    dw_down[...] += dot(g_low, act[...], NT)
    for first in range(0, hidden_units, UNITS):
        span = slice(first, first + UNITS)
        act[span, :] = (dot(down_t[span, :], g_low) * slope[span, :]).astype(bf16)
    c_grad = dot(w_up[...], act[...])
    dw_up[...] += dot(c_low, act[...], NT)
    for part in range(hidden_units // model):
        dvec[:, 3 + part : 4 + part] += lane_sum(act[part * model : (part + 1) * model, :].astype(f32))

    @pl.when(step == pl.num_programs(0) - 1)
    def _():
        is_first = lax.axis_index("core") == 0
        for side, (low, here, there, out) in enumerate(
            ((down_t, dw_down, dw_up, send_pair), (up_t, dw_up, dw_down, keep_pair))
        ):
            for part in range(chunks):
                span = slice(part * unit, (part + 1) * unit)
                low[part * model : (part + 1) * model, :] = jnp.where(is_first, here[:, span], there[:, span]).astype(bf16)
            pltpu.make_async_copy(low, out, sems.at[side]).start()

    dvec[:, 1:2] += lane_sum(c_grad * hat_two)
    dvec[:, 2:3] += lane_sum(c_grad)
    x1_grad = x2_grad + norm_back(c_grad, hat_two, inverse_two, col(6))
    dx1[...] = x1_grad
    x1_low = x1_grad.astype(bf16)
    dvec[:, 0:1] += lane_sum(x1_low.astype(f32))
    dw_out[0:model, :] += dot(attended[...], x1_low, NT)
    o_grad = dot(w_out[...], x1_low)
    inner = o_grad * attended[...].astype(f32)
    row = rows_of(EXT - HEAD_DIM, width)
    for head in range(heads):
        span = slice(head * HEAD_DIM, (head + 1) * HEAD_DIM)
        share = inverse[head, 0:1, :]
        high, middle, rest = split3(-jnp.sum(inner[span, :], axis=0, keepdims=True) * share)
        do_ext[head, 0:HEAD_DIM, :] = (o_grad[span, :] * share).astype(bf16)
        tail = jnp.where(row == 0, high, jnp.where(row == 1, middle, jnp.where(row == 2, rest, 0.0)))
        do_ext[head, HEAD_DIM:EXT, :] = tail.astype(bf16)

    @pl.when(step == pl.num_programs(0) - 1)
    def _():
        dw_out[model:, :] = dvec[...].T
        split_halves(dw_out, keep_rest, send_rest)
        for side, (low, out) in enumerate(((down_t, send_pair), (up_t, keep_pair))):
            pltpu.make_async_copy(low, out, sems.at[side]).wait()


def chunks_of_bias(model):
    return FF // model


def input_back_kernel(meta, x0, dq, dk, dv, dx1, weight, vectors, dtable_in, *rest, last):
    if last:
        loss, dvec_in, tail, vec, wide, dvec, dtable = rest
    else:
        dvec, dtable, vec, wide = rest
    step = pl.program_id(0)
    model, width = x0.shape

    @pl.when(step == 0)
    def _():
        vec[...] = columns_of(vectors, wide)
        dtable[...] = dtable_in[...]
        dvec[...] = dvec_in[...] if last else jnp.zeros_like(dvec)

    back = None
    for part, grad in enumerate((dq, dk, dv)):
        share = dot(weight[:, part * model : (part + 1) * model], grad[...])
        back = share if back is None else back + share
    hat, inverse = norm_stats(x0[...])
    dvec[:, 0:1] += lane_sum(back * hat)
    dvec[:, 1:2] += lane_sum(back)
    dvec[0:1, 2:3] += lane_sum(meta[4:5, :])
    x0_grad = dx1[...] + norm_back(back, hat, inverse, vec[:, 0:1])
    onehot = (rows_of(VPAD, width) == meta[0:1, :].astype(jnp.int32)).astype(f32).astype(bf16)
    high = x0_grad.astype(bf16)
    for piece in (high, (x0_grad - high.astype(f32)).astype(bf16)):
        dtable[...] += dot(onehot, piece, NT)

    if last:

        @pl.when(step == pl.num_programs(0) - 1)
        def _():
            columns = dvec[...].T[0:8, :]
            tail[0:VOCAB_ROWS, 0:model] = dtable[0:VOCAB_ROWS, :]
            tail[VOCAB_ROWS:, 0:model] = jnp.where(rows_of(8, model) < 2, columns, 0.0)
            lane = lax.broadcasted_iota(jnp.int32, (TAIL, 128), 1)
            numbers = jnp.where(lane == 0, loss[0:1, 0:1], jnp.where(lane == 1, columns[2:3, 0:1], 0.0))
            tail[:, model:] = jnp.where(rows_of(TAIL, 128) == 0, numbers, 0.0)


def encode(tail):
    wide = tail.shape[1] - 128
    row = rows_of(tail.shape[0], 128)
    high, middle, rest = split3(tail[0:1, wide:])
    scalars = jnp.where(row == 0, high, jnp.where(row == 1, middle, jnp.where(row == 2, rest, 0.0)))
    return jnp.concatenate([tail[:, :wide], scalars], axis=1)


def decode(tail):
    wide = tail.shape[1] - 128
    row = rows_of(tail.shape[0], 128)
    total = tail[0:1, wide:] + tail[1:2, wide:] + tail[2:3, wide:]
    return jnp.concatenate([tail[:, :wide], jnp.where(row == 0, total, 0.0)], axis=1)


def pack_kernel(swapped, pair, tail, out, keep, send, *, pieces):
    shares = swapped[...].astype(f32)
    rows = shares.shape[0] // pieces
    total = None
    for at in range(pieces):
        share = shares[at * rows : (at + 1) * rows, :]
        total = share if total is None else total + share
    both = pair[...].astype(f32)
    half = keep.shape[0]
    first, second = both[0:half, :], both[half:, :]
    square = jnp.sum(lane_sum(first * first + second * second), axis=0, keepdims=True)
    is_first = lax.axis_index("core") == 0
    keep[...] = jnp.where(is_first, first, second).astype(bf16)
    send[...] = jnp.where(is_first, second, first).astype(bf16)
    values = tail[...]
    wide = values.shape[1] - 128
    at_square = (rows_of(values.shape[0], 128) == 0) & (lax.broadcasted_iota(jnp.int32, (values.shape[0], 128), 1) == 2)
    values = jnp.concatenate([values[:, :wide], values[:, wide:] + jnp.where(at_square, square, 0.0)], axis=1)
    out[...] = jnp.concatenate([total, encode(values)], axis=0).astype(bf16)


def stage_kernel(own, one, two, three, out, *, axis):
    index = lax.axis_index(axis)
    odd, high = lax.rem(index, 2) == 1, index >= 2
    values = [ref[...].astype(f32) for ref in (own, one, two, three)]
    rows = values[0].shape[0] - TAIL
    parts = [value[0:rows, :] for value in values]
    near = jnp.where(odd, parts[1], parts[0]), jnp.where(odd, parts[0], parts[1])
    far = jnp.where(odd, parts[3], parts[2]), jnp.where(odd, parts[2], parts[3])
    placed = [jnp.where(high, far[i], near[i]) for i in range(2)] + [jnp.where(high, near[i], far[i]) for i in range(2)]
    tails = [decode(value[rows:, :]) for value in values]
    total = (tails[0] + tails[1]) + (tails[2] + tails[3])
    out[...] = jnp.concatenate([*placed, encode(total)], axis=0).astype(bf16)


def adam_step(weight, grad, drift, spread, rate):
    drift = FIRST_DECAY * drift + (1.0 - FIRST_DECAY) * grad
    spread = SECOND_DECAY * spread + (1.0 - SECOND_DECAY) * grad * grad
    adjusted = (
        drift
        / (1.0 - FIRST_DECAY**STEP)
        / (jnp.sqrt(spread / (1.0 - SECOND_DECAY**STEP)) + ADAM_EPS)
    )
    return (weight - rate * (adjusted + WEIGHT_DECAY * weight), drift, spread)


def update_kernel(*refs, groups, early_groups):
    early_mine, early_other, last_mine, last_other, pair_keep, pair_sent = refs[:6]
    ins, outs = refs[6:21], refs[21:41]
    pair_out, norm_out, g_in, g_out, g_table, g_vec, scale, sems = refs[41:49]
    held = refs[49:]
    step = pl.program_id(0)
    steps = g_in.shape[0] // outs[4].shape[0]

    def copy(array, chunk):
        span = pl.ds(chunk * outs[4].shape[0], outs[4].shape[0])
        return pltpu.make_async_copy(ins[3 + array].at[span], held[array].at[span], sems.at[array, chunk])

    @pl.when(step == 0)
    def _():
        for chunk in range(steps):
            for array in range(6):
                copy(array, chunk).start()

    vocab, model = ins[0].shape
    half_rows = early_mine.shape[0]
    piece = model // groups
    after = model - half_rows

    @pl.when(step == 0)
    def _():
        is_first = lax.axis_index("core") == 0

        def halves(mine, other):
            mine, other = mine[0:half_rows, :].astype(f32), other[0:half_rows, :].astype(f32)
            return jnp.where(is_first, mine, other), jnp.where(is_first, other, mine)

        squares = jnp.zeros((1, 128), f32)

        def add_squares(values):
            rows = jnp.sum(values * values, axis=0, keepdims=True)
            total = None
            for at in range(0, rows.shape[1], 128):
                total = rows[:, at : at + 128] if total is None else total + rows[:, at : at + 128]
            return total

        for mine, other, first, size in (
            (early_mine, early_other, 0, early_groups),
            (last_mine, last_other, early_groups, groups - early_groups),
        ):
            upper, lower = halves(mine, other)
            if first == 0:
                rest_upper, rest_lower = upper[:, 3 * piece * size :], lower[:, 3 * piece * size :]
            upper, lower = upper[:, : 3 * piece * size], lower[:, : 3 * piece * size]
            squares += add_squares(upper) + add_squares(lower)
            for group in range(size):
                for part in range(3):
                    source = slice((group * 3 + part) * piece, (group * 3 + part + 1) * piece)
                    at = part * model + (first + group) * piece
                    g_in[0:half_rows, at : at + piece] = upper[:, source]
                    g_in[half_rows:model, at : at + piece] = lower[0:after, source]
                    into = slice((first + group) * piece, (first + group + 1) * piece)
                    g_vec[2 + part : 3 + part, into] = lower[after : after + 1, source]
        upper, lower = rest_upper, rest_lower
        g_out[0:half_rows, :] = upper
        g_out[half_rows:, :] = lower[0:after, :]
        others = lower[after : after + 16, :]
        g_vec[5:15, :] = others[0:10, :]
        tails = [decode(ref[half_rows:, :].astype(f32)) for ref in (last_mine, last_other)]
        final = tails[0] + tails[1]
        scalars = final[:, model:]
        table = final[0:VOCAB_ROWS, 0:model]
        g_table[...] = table
        tail = final[VOCAB_ROWS:, 0:model]
        g_vec[0:2, :] = tail[0:2, :]
        squares += add_squares(upper) + add_squares(lower[0:after, :]) + add_squares(others) + add_squares(table)
        squares += add_squares(tail[0:2, :])
        total = lane_sum(squares) + scalars[0:1, 2:3]
        crops = scalars[0:1, 1:2]
        norm = jnp.sqrt(total) / crops
        scale[...] = jnp.broadcast_to(jnp.minimum(1.0, CLIP_NORM / (norm + 1e-06)) / crops, scale.shape)
        pair_out[0] = jnp.sum(scalars[0:1, 0:1])
        pair_out[1] = jnp.sum(crops)
        norm_out[0] = jnp.sum(norm)

    factor = scale[0:1, 0:1]

    def update(which, grad, rate, span=...):
        source = held[which * 3 - 3 : which * 3] if span is not ... else ins[which * 3 : which * 3 + 3]
        weight, drift, spread = (ref[span] for ref in source)
        fresh, drift, spread = adam_step(weight, grad * factor, drift, spread, rate)
        out = outs[which * 4 : which * 4 + 4]
        out[0][...] = fresh
        out[1][...] = drift
        out[2][...] = spread
        out[3][...] = fresh.astype(bf16)

    @pl.when(step == 0)
    def _():
        update(0, g_table[0:vocab, :], 0.05)
        keep, sent = pair_keep[...].astype(f32), pair_sent[...].astype(f32)
        is_first = lax.axis_index("core") == 0
        update(3, jnp.stack([jnp.where(is_first, keep, sent), jnp.where(is_first, sent, keep)]), 0.05)
        update(4, g_vec[0:15, :], 0.2)

    for array in range(6):
        copy(array, step).wait()
    rows = outs[4].shape[0]
    span = pl.ds(pl.multiple_of(step * rows, rows), rows)
    update(1, g_in[span, :], 0.05, span)
    update(2, g_out[span, :], 0.1, span)


def whole(shape):
    return pl.BlockSpec(shape, lambda *_: (0,) * len(shape), pipeline_mode=pl.Buffered(1))


def shaped(shape, dtype):
    return jax.ShapeDtypeStruct(shape, dtype)


def limits(mib):
    return pltpu.CompilerParams(vmem_limit_bytes=mib * MIB)


def cost(flops, moved, transcendentals=0):
    return pl.CostEstimate(flops=int(flops), bytes_accessed=int(moved), transcendentals=int(transcendentals))


def rotary_constants(rows):
    freq = np.float32(10000.0) ** (-np.arange(0, HEAD_DIM, 2, dtype=np.float32) / np.float32(HEAD_DIM))
    angle = np.arange(rows, dtype=np.float32)[None, :] * freq[:, None].astype(np.float32)
    return np.cos(angle).astype(np.float32), np.sin(angle).astype(np.float32)


def body(
    columns,
    deep,
    true_ids,
    picked,
    replace_kinds,
    random_ids,
    splits,
    embedding,
    projection,
    outward,
    feedforward,
    vectors,
    embedding_drift,
    embedding_spread,
    projection_drift,
    projection_spread,
    outward_drift,
    outward_spread,
    feedforward_drift,
    feedforward_spread,
    vectors_drift,
    vectors_spread,
):
    tokens = true_ids.shape[0]
    slots = splits.shape[0]
    rows = tokens // slots
    half = rows // 2
    vocab, model = embedding.shape
    heads = model // HEAD_DIM
    bias_rows = chunks_of_bias(model)
    block = half
    blocks = tokens // block
    wide = FF // columns
    devices = columns * deep * 2
    chips = ("col", "deep")
    everywhere = ("col", "deep", "core")

    pair_all = lax.all_gather(feedforward.astype(bf16), everywhere, axis=1, tiled=True)
    pair_all = pair_all.reshape(2, columns, model, wide)

    cos_np, sin_np = rotary_constants(rows)
    cos_table, sin_table = jnp.asarray(cos_np), jnp.asarray(sin_np)
    twice_cos, twice_sin = (jnp.asarray(np.tile(t[:, :half], (1, 2))) for t in (cos_np, sin_np))

    def by_block(count):
        return pl.BlockSpec((count, block), lambda i: (0, i))

    def heads_block(count):
        return pl.BlockSpec((heads, count, block), lambda i: (0, 0, i))

    first_half = pl.BlockSpec((HALF, block), lambda i: (0, 0))
    own_half = pl.BlockSpec((HALF, block), lambda i: (0, i % 2))
    id_block = pl.BlockSpec((1, block), lambda i: (0, i))
    meta, x0, normed, q_ext, k_ext, v_ext, qkv_low = pl.pallas_call(
        qkv_kernel,
        grid=(blocks,),
        in_specs=[id_block] * 4 + [pl.BlockSpec((1, rows), lambda i: (0, i // 2)), pl.BlockSpec(memory_space=pltpu.SMEM),
                  whole((vocab, model)), whole((model, 3 * model)), whole(vectors.shape),
                  first_half, own_half, first_half, own_half],
        out_specs=[by_block(8), by_block(model), by_block(model + 16), heads_block(EXT), heads_block(EXT), heads_block(EXT),
                   whole((model, 3 * model))],
        out_shape=[shaped((8, tokens), f32), shaped((model, tokens), f32), shaped((model + 16, tokens), bf16)]
        + [shaped((heads, EXT, tokens), bf16)] * 3 + [shaped((model, 3 * model), bf16)],
        scratch_shapes=[pltpu.VMEM((model, 128), bf16), pltpu.VMEM((3 * model, model), bf16), pltpu.VMEM((model, 128), f32),
                        pltpu.VMEM((128, model), f32)],
        compiler_params=limits(56),
        cost_estimate=cost(2 * 3 * model * model * tokens, 20 * model * tokens),
        name="embed_and_qkv",
    )(*(ids.reshape(1, tokens) for ids in (true_ids, picked, replace_kinds, random_ids, picked)), splits,
      embedding, projection, vectors, cos_table, cos_table, sin_table, sin_table)

    per = 4

    def head_group(count, size, first=0):
        return pl.BlockSpec((size, count, rows), lambda s, g: (first + g, 0, s))

    attended, raised, inverse = pl.pallas_call(
        attention_kernel,
        grid=(slots, heads // per),
        in_specs=[head_group(EXT, per)] * 3,
        out_specs=[head_group(HEAD_DIM, per), pl.BlockSpec((per, rows, rows), lambda s, g: (g, s, 0)), head_group(8, per)],
        out_shape=[shaped((heads, HEAD_DIM, tokens), bf16), shaped((heads, tokens, rows), bf16), shaped((heads, 8, tokens), f32)],
        compiler_params=limits(56),
        cost_estimate=cost(2 * 16 * model * rows * tokens, 2 * heads * rows * tokens, heads * rows * tokens),
        name="attention",
    )(q_ext, k_ext, v_ext)
    attended = attended.reshape(model, tokens)

    half_rows = (model + 128) // 2
    owned = -(-half_rows // (8 * columns * deep)) * 8
    dx1, do_ext, keep_pair, send_pair, keep_rest, send_rest, dtable_end, loss = pl.pallas_call(
        middle_kernel,
        grid=(blocks,),
        in_specs=[by_block(8), by_block(model), by_block(model), heads_block(8), whole((model, model)),
                  pl.BlockSpec(memory_space=pl.ANY), whole((vocab, model)), whole(vectors.shape)],
        out_specs=[by_block(model), heads_block(EXT), pl.BlockSpec(memory_space=pl.ANY), pl.BlockSpec(memory_space=pl.ANY),
                   whole((half_rows, model)), whole((half_rows, model)), whole((VPAD, model)), whole((8, 128))],
        out_shape=[shaped((model, tokens), f32), shaped((heads, EXT, tokens), bf16), shaped((columns * model, wide), bf16),
                   shaped((columns * model, wide), bf16), shaped((half_rows, model), bf16), shaped((half_rows, model), bf16),
                   shaped((VPAD, model), f32), shaped((8, 128), f32)],
        scratch_shapes=[pltpu.VMEM((model, FF), bf16), pltpu.VMEM((model, FF), bf16), pltpu.VMEM((FF, model), bf16),
                        pltpu.VMEM((FF, model), bf16), pltpu.VMEM((FF, block), bf16), pltpu.VMEM((FF, block), bf16),
                        pltpu.VMEM((model, FF), f32), pltpu.VMEM((model, FF), f32),
                        pltpu.VMEM((model + 128, model), f32), pltpu.VMEM((model, 128), f32),
                        pltpu.VMEM((model, 128), f32), pltpu.VMEM((128, model), f32),
                        pltpu.VMEM((VPAD, model), bf16), pltpu.VMEM((model, 128), bf16),
                        pltpu.VMEM((model, model), bf16), pltpu.VMEM((model, model), bf16), pltpu.SemaphoreType.DMA((2 + 2 * columns,))],
        compiler_params=limits(62),
        cost_estimate=cost(2 * tokens * model * (6 * FF + 3 * model), 14 * model * tokens + 16 * model * FF, FF * tokens),
        name="feedforward_and_head",
    )(meta, x0, attended, inverse, outward, pair_all, embedding, vectors)

    count = columns * deep

    def swap(values, axes):
        return lax.all_to_all(values, axes, 0, 0, tiled=True)

    def over_core(values):
        return lax.ppermute(values, "core", [(0, 1), (1, 0)])

    def add_up(values, pieces):
        return jnp.sum(values.reshape((pieces, -1) + values.shape[1:]).astype(f32), axis=0)

    def pair_sum(keep, sent):
        return (keep.astype(f32) + sent.astype(f32)).astype(bf16)

    def pad_rows(values):
        return jnp.pad(values, ((0, owned * count - half_rows), (0, 0)))

    def to_owner(values):
        return swap(pad_rows(values), chips)

    def gather4(values, axis):
        one, two, three = (lax.ppermute(values, axis, [(i, i ^ d) for i in range(4)]) for d in (1, 2, 3))
        index = lax.axis_index(axis)
        odd, high = index % 2 == 1, index >= 2
        near = jnp.where(odd, one, values), jnp.where(odd, values, one)
        far = jnp.where(odd, three, two), jnp.where(odd, two, three)
        return jnp.concatenate(
            [jnp.where(high, far[i], near[i]) for i in range(2)] + [jnp.where(high, near[i], far[i]) for i in range(2)],
            axis=0,
        )

    def gather_deep(values):
        return gather4(values, "deep") if deep == 4 else lax.all_gather(values, "deep", axis=0, tiled=True)

    def gather_col(values):
        return (gather4(values, "col") if columns == 4 else lax.all_gather(values, "col", axis=0, tiled=True))[:half_rows]

    def together(first, *others):
        return lax.optimization_barrier((first, *others))

    pair_sent, rest_sent = over_core(send_pair), over_core(send_rest)
    per_call = 4
    width = 3 * per_call * HEAD_DIM
    grads = None
    keeps, sents = [], []
    groups = heads // per_call
    calls = [(0, 0, 1), (0, 1, slots - 1)] + [(g, 0, slots) for g in range(1, groups)]
    carry = None
    for index, (first, from_slot, slot_count) in enumerate(calls):
        chained, carried, finished = grads is not None, carry is not None, from_slot + slot_count == slots

        def group(count, first=first, from_slot=from_slot):
            return pl.BlockSpec((per_call, count, rows), lambda s: (first, 0, from_slot + s))

        def by_slot(count, from_slot=from_slot):
            return pl.BlockSpec((count, rows), lambda s: (0, from_slot + s))

        table_spec = pl.BlockSpec((HALF, rows), lambda s: (0, 0))
        outs = pl.pallas_call(
            functools.partial(attention_back_kernel, chunk=half, chained=chained, carried=carried, finished=finished,
                              first_head=first * per_call, from_slot=from_slot),
            grid=(slot_count,),
            in_specs=[group(EXT)] * 4 + [pl.BlockSpec(memory_space=pl.ANY), by_slot(model + 16), by_slot(8)] + [table_spec] * 4
            + [pl.BlockSpec(memory_space=pl.ANY)] * (3 if chained else 0)
            + ([whole((2 * half_rows, width))] if carried else []),
            out_specs=[group(HEAD_DIM)] * 3
            + ([pl.BlockSpec((half_rows, width), lambda s: (0, 0))] * 2 if finished else [whole((2 * half_rows, width))]),
            out_shape=[shaped((heads, HEAD_DIM, tokens), bf16)] * 3
            + ([shaped((half_rows, width), bf16)] * 2 if finished else [shaped((2 * half_rows, width), f32)]),
            scratch_shapes=[pltpu.VMEM((width, rows), bf16), pltpu.VMEM((slot_count * per_call, rows, rows), bf16),
                            pltpu.SemaphoreType.DMA((slot_count * per_call,))]
            + ([pltpu.VMEM((2 * half_rows, width), f32)] if finished else []),
            input_output_aliases={11: 0, 12: 1, 13: 2} if chained else {},
            compiler_params=limits(56),
            cost_estimate=cost(2 * 40 * width // 3 * rows * rows * slot_count, 20 * width * rows * slot_count, per_call * rows * rows * slot_count),
            name="attention_back",
        )(q_ext, k_ext, v_ext, do_ext, raised, normed, meta, twice_cos, cos_table, twice_sin, sin_table, *(grads or ()),
          *((carry,) if carried else ()))
        grads = list(outs[:3])
        carry = None if finished else outs[3]
        if finished:
            keeps.append(outs[3])
            sents.append(over_core(outs[4]))
        if index == 0:
            grads[0], pair_sent, rest_sent = together(grads[0], pair_sent, rest_sent)
            pair = pair_sum(keep_pair.reshape(count, -1, wide), pair_sent.reshape(count, -1, wide))
            rest_half = pad_rows(pair_sum(keep_rest, rest_sent)).reshape(count, owned, model)
            pair = jnp.concatenate([pair, rest_half], axis=1).reshape(-1, wide)
            do_ext, pair = together(do_ext, pair)
            pair = lax.psum_scatter(pair, "col", scatter_dimension=0, tiled=True)
        elif first == groups - 3:
            do_ext, pair = together(do_ext, pair)
            pair = lax.psum_scatter(pair, "deep", scatter_dimension=0, tiled=True)
        elif first == groups - 2:
            early = jnp.concatenate([pair_sum(keeps[i], sents[i]) for i in range(groups - 2)], axis=1)
            do_ext, early = together(do_ext, early)
            early = to_owner(early)
        elif first == groups - 1:
            late_half = jnp.concatenate([pair_sum(keeps[i], sents[i]) for i in range(groups - 2, groups)], axis=1)
            early = add_up(early, count).astype(bf16)
            dx1, late_half, early, pair = together(dx1, late_half, early, pair)
            late_half = to_owner(late_half)
            early = gather_deep(jnp.concatenate([early, pair[-owned:]], axis=1))
            pair = pair[:-owned]
    dq, dk, dv = (grad.reshape(model, tokens) for grad in grads)

    back_out = [shaped((model, 128), f32), shaped((VPAD, model), f32)]
    back_room = [pltpu.VMEM((model, 128), f32), pltpu.VMEM((128, model), f32)]

    def input_back(part, extra):
        def by_part(rows_):
            return pl.BlockSpec((rows_, block), lambda i: (0, i + part * (blocks // 2)))

        last = part == 1
        room = [pltpu.VMEM(shape.shape, f32) for shape in back_out]
        return pl.pallas_call(
            functools.partial(input_back_kernel, last=last),
            grid=(blocks // 2,),
            in_specs=[by_part(8)] + [by_part(model)] * 5 + [whole((model, 3 * model)), whole(vectors.shape)]
            + [whole(array.shape) for array in extra],
            out_specs=[whole((TAIL, model + 128))] if last else [whole(shape.shape) for shape in back_out],
            out_shape=[shaped((TAIL, model + 128), f32)] if last else back_out,
            scratch_shapes=back_room + (room if last else []),
            compiler_params=limits(56),
            cost_estimate=cost(model * model * tokens, 4 * model * tokens),
            name="input_back",
        )(meta, x0, dq, dk, dv, dx1, qkv_low, vectors, *extra)

    halfway = input_back(0, (dtable_end,))
    dvec_half, dtable_half, early = together(*halfway, early)
    early = gather_col(early)
    (tail,) = input_back(1, (dtable_half, loss, dvec_half))
    tail, pair, early, late_half = together(tail, pair, early, late_half)
    early_other = over_core(early)

    def call_small(kernel, args, outs, name):
        return pl.pallas_call(
            kernel,
            in_specs=[pl.BlockSpec(memory_space=pltpu.VMEM)] * len(args),
            out_specs=[pl.BlockSpec(memory_space=pltpu.VMEM)] * len(outs),
            out_shape=[shaped(shape, bf16) for shape in outs],
            compiler_params=limits(40),
            cost_estimate=cost(1e6, 4e6),
            name=name,
        )(*args)

    own = pair.shape[0] // 2
    last_width = late_half.shape[1]
    if columns == 4 and deep == 4 and last_width == tail.shape[1]:
        packed, pair_keep, pair_sent = call_small(
            functools.partial(pack_kernel, pieces=count), (late_half, pair, tail),
            [(owned + TAIL, last_width), (own, wide), (own, wide)], "pack",
        )
        pair_sent = over_core(pair_sent)
        for axis in ("deep", "col"):
            got = [lax.ppermute(packed, axis, [(i, i ^ d) for i in range(4)]) for d in (1, 2, 3)]
            merged = 4 * (packed.shape[0] - TAIL) + TAIL
            (packed,) = call_small(functools.partial(stage_kernel, axis=axis), (packed, *got), [(merged, last_width)], "stage")
    else:
        is_first = lax.axis_index("core") == 0
        pair_keep = jnp.where(is_first, pair[:own], pair[own:])
        pair_sent = over_core(jnp.where(is_first, pair[own:], pair[:own]))
        square = jnp.sum(jnp.square(pair.astype(f32)))
        tail = lax.psum(tail.at[0, model + 2].add(square), chips)
        scalars = tail[0:1, model:]
        high = lax.reduce_precision(scalars, 8, 7)
        middle = lax.reduce_precision(scalars - high, 8, 7)
        numbers = jnp.concatenate([high, middle, scalars - high - middle, jnp.zeros((TAIL - 3, 128), f32)], axis=0)
        tail = jnp.pad(jnp.concatenate([tail[:, :model], numbers], axis=1), ((0, 0), (0, last_width - tail.shape[1])))
        packed = gather_col(gather_deep(add_up(late_half, count).astype(bf16)))
        packed = jnp.concatenate([packed, tail.astype(bf16)], axis=0)
    packed_other = over_core(packed)

    steps = 10
    state = (
        (embedding, embedding_drift, embedding_spread),
        (projection, projection_drift, projection_spread),
        (outward, outward_drift, outward_spread),
        (feedforward, feedforward_drift, feedforward_spread),
        (vectors, vectors_drift, vectors_spread),
    )

    def state_spec(array):
        if array.shape[0] == model:
            return pl.BlockSpec((model // steps, array.shape[1]), lambda i: (i, 0))
        return whole(array.shape)

    grads_in = (early, early_other, packed, packed_other, pair_keep, pair_sent)
    results = pl.pallas_call(
        functools.partial(update_kernel, groups=groups, early_groups=groups - 2),
        grid=(steps,),
        in_specs=[whole(array.shape) for array in grads_in] + [
            pl.BlockSpec(memory_space=pl.ANY) if array.shape[0] == model else whole(array.shape) for three in state for array in three
        ],
        out_specs=[state_spec(three[0]) for three in state for _ in range(4)]
        + [pl.BlockSpec(memory_space=pltpu.SMEM)] * 2,
        out_shape=[shaped(three[0].shape, dtype) for three in state for dtype in (f32, f32, f32, bf16)]
        + [shaped((2,), f32), shaped((1,), f32)],
        scratch_shapes=[pltpu.VMEM((model, 3 * model), f32), pltpu.VMEM((model, model), f32), pltpu.VMEM((VOCAB_ROWS, model), f32),
                        pltpu.VMEM((16, model), f32), pltpu.VMEM((8, 128), f32), pltpu.SemaphoreType.DMA((6, steps))]
        + [pltpu.VMEM(array.shape, f32) for three in state[1:3] for array in three],
        compiler_params=limits(56),
        cost_estimate=cost(60 * 4 * model * model, 4 * 30 * model * model),
        name="clip_and_adamw",
    )(*grads_in, *(array for three in state for array in three))
    return (results[20], results[21].reshape(()), *results[:20])


def solution(mesh):
    columns, row = mesh.shape["col"], mesh.shape["row"]
    fine = jax.sharding.Mesh(mesh.devices.reshape(columns, row // 2, 2), ("col", "deep", "core"))
    split_all, tiles, full = P(("col", "deep", "core")), P(None, ("deep", "core"), "col"), P()
    return jax.shard_map(
        functools.partial(body, columns, row // 2),
        mesh=fine,
        in_specs=(split_all,) * 5 + (full,) * 3 + (tiles,) + (full,) * 7 + (tiles,) * 2 + (full,) * 2,
        out_specs=(full,) * 14 + (tiles,) * 4 + (full,) * 4,
        check_vma=False,
    )
```

```python
import functools
import math

import jax
import jax.numpy as jnp
import numpy as np
from jax import lax
from jax.experimental import pallas as pl
from jax.experimental.pallas import tpu as pltpu
from jax.sharding import PartitionSpec as P

HEAD_DIM = 32
HALF = HEAD_DIM // 2
EXT = HEAD_DIM + 16
FF = 2560
STEP = 10
VPAD = 48
VOCAB_ROWS = 40
TAIL = 48
UNITS = 640
THIRD = 40

EPS_NORM = 1e-05
CLIP_NORM = 0.002
FIRST_DECAY = 0.5
SECOND_DECAY = 0.5
ADAM_EPS = 1e-08
WEIGHT_DECAY = 0.01
MASK_ID = 32
MASKED = 1e30
SAFE_EXPONENT = 40.0

LOG2E = math.log2(math.e)
SCALE = HEAD_DIM ** (-0.5)
MIB = 2**20

bf16 = jnp.bfloat16
f32 = jnp.float32

NN = ((1,), (0,))
NT = ((1,), (1,))
TN = ((0,), (0,))


def dot(left, right, dims=NN):
    return lax.dot_general(left, right, (dims, ((), ())), preferred_element_type=f32)


def split3(values):
    high = values.astype(bf16).astype(f32)
    rest = values - high
    middle = rest.astype(bf16).astype(f32)
    return high, middle, rest - middle


def norm_stats(values):
    center = values - jnp.mean(values, axis=0, keepdims=True)
    inverse = lax.rsqrt(jnp.mean(center * center, axis=0, keepdims=True) + EPS_NORM)
    return center * inverse, inverse


def norm_back(grad, hat, inverse, gain):
    scaled = grad * gain
    return inverse * (
        scaled
        - jnp.mean(scaled, axis=0, keepdims=True)
        - hat * jnp.mean(scaled * hat, axis=0, keepdims=True)
    )


def rows_of(count, width):
    return lax.broadcasted_iota(jnp.int32, (count, width), 0)


def split_halves(total, keep, send):
    rows = keep.shape[0]
    first, second = total[0:rows, :], total[rows:, :]
    is_first = lax.axis_index("core") == 0
    keep[...] = jnp.where(is_first, first, second).astype(bf16)
    send[...] = jnp.where(is_first, second, first).astype(bf16)


def lane_sum(values):
    return jnp.sum(values, axis=1, keepdims=True)


def columns_of(vectors, wide):
    wide[...] = jnp.zeros_like(wide)
    wide[0 : vectors.shape[0], :] = vectors[...]
    return wide[...].T


def qkv_kernel(
    true_ids, picked, kinds, random_ids, slot_picked, splits, embedding, projection, vectors, cos_a, cos_b, sin_a, sin_b,
    meta, x0, low, q_ext, k_ext, v_ext, rounded,
    table, weight, vec, wide,
):
    width = true_ids.shape[1]
    heads = q_ext.shape[0]
    model = x0.shape[0]
    vocab = embedding.shape[0]
    block = pl.program_id(0)

    @pl.when(pl.program_id(0) == 0)
    def _():
        vec[...] = columns_of(vectors, wide)
        wide[...] = jnp.zeros_like(wide)
        for part, piece in enumerate(split3(embedding[...])):
            wide[part * THIRD : part * THIRD + vocab, :] = piece
        table[...] = wide[...].T.astype(bf16)
        for part in range(3):
            span = slice(part * model, (part + 1) * model)
            rounded[:, span] = projection[:, span].astype(bf16)
            weight[span, :] = rounded[:, span].T

    is_pick = picked[...] == 1
    masked, swapped = is_pick & (kinds[...] < 8), is_pick & (kinds[...] == 8)
    ids = jnp.where(masked, MASK_ID, jnp.where(swapped, random_ids[...], true_ids[...]))
    split = splits[block // 2]
    second = jnp.full((1, width), split * (block % 2), jnp.int32).astype(f32)
    picks = picked[...].astype(f32)
    counts = lane_sum(jnp.where(split > 0, picks, 0.0))
    counts += lane_sum(jnp.where(split > 0, 0.0, slot_picked[...].astype(f32)))
    crop_share = jnp.full((1, width), 1 + split, jnp.int32).astype(f32) * (1.0 / slot_picked.shape[1])
    at = rows_of(8, width)
    rows = jnp.where(at == 0, ids.astype(f32), jnp.where(at == 1, true_ids[...].astype(f32), jnp.where(at == 2, second, 0.0)))
    meta[...] = jnp.where(at == 3, picks / counts, jnp.where(at == 4, crop_share, rows))
    vocab3 = rows_of(128, width)
    onehot = ((vocab3 == ids) | (vocab3 == ids + THIRD) | (vocab3 == ids + 2 * THIRD)).astype(f32).astype(bf16)
    embedded = dot(table[...], onehot)
    x0[...] = embedded
    hat, _ = norm_stats(embedded)
    normed = (hat * vec[:, 0:1] + vec[:, 1:2]).astype(bf16)
    row = rows_of(EXT - HEAD_DIM, width)
    low[0:model, :] = normed
    low[model : model + 16, :] = jnp.where(row == 0, 1.0, 0.0).astype(bf16)
    in_second = second > 0.5
    cos = jnp.where(in_second, cos_a[...], cos_b[...])
    sin = jnp.where(in_second, sin_a[...], sin_b[...])
    q_rows = jnp.where(row == 0, second, jnp.where(row == 1, 1.0 - second, 0.0)).astype(bf16)
    k_rows = jnp.where(
        row == 0,
        -MASKED * (1.0 - second),
        jnp.where(row == 1, -MASKED * second, jnp.where(row < 5, 1.0, 0.0)),
    ).astype(bf16)
    v_rows = jnp.where(row < 3, 1.0, 0.0).astype(bf16)
    for part, out, extra in ((0, q_ext, q_rows), (1, k_ext, k_rows), (2, v_ext, v_rows)):
        base = part * model
        mixed = dot(weight[base : base + model, :], normed) + vec[:, 2 + part : 3 + part]
        for head in range(heads):
            one = mixed[head * HEAD_DIM : head * HEAD_DIM + HALF, :]
            two = mixed[head * HEAD_DIM + HALF : (head + 1) * HEAD_DIM, :]
            if part < 2:
                one, two = one * cos - two * sin, two * cos + one * sin
            out[head, 0:HALF, :] = one.astype(bf16)
            out[head, HALF:HEAD_DIM, :] = two.astype(bf16)
            out[head, HEAD_DIM:EXT, :] = extra


def attention_kernel(q_ext, k_ext, v_ext, out, raised, inverse):
    heads, _, width = q_ext.shape
    factor = LOG2E * SCALE

    def longest(array):
        values = array[:, 0:HEAD_DIM, :].astype(f32)
        return jnp.max(jnp.sum(values * values, axis=1))

    def finish(head):
        mixed = dot(v_ext[head], raised[head], NT)
        share = 1.0 / mixed[HEAD_DIM : HEAD_DIM + 1, :]
        out[head] = (mixed[0:HEAD_DIM, :] * share).astype(bf16)
        inverse[head] = jnp.broadcast_to(share, (8, width))

    small = longest(q_ext) * longest(k_ext) * factor**2 <= SAFE_EXPONENT**2

    @pl.when(small)
    def _():
        for head in range(heads):
            raised[head] = jnp.exp2(dot(q_ext[head], k_ext[head], TN) * factor).astype(bf16)
            finish(head)

    @pl.when(jnp.logical_not(small))
    def _():
        for head in range(heads):
            scores = dot(q_ext[head], k_ext[head], TN)
            top = jnp.max(scores, axis=1, keepdims=True)
            raised[head] = jnp.exp2((scores - top) * factor).astype(bf16)
            finish(head)


def attention_back_kernel(
    q_ext, k_ext, v_ext, do_ext, raised, low, meta, cos_a, cos_b, sin_a, sin_b, *rest,
    chunk, chained, carried, finished, first_head, from_slot,
):
    rest = list(rest[3:] if chained else rest)
    before = rest.pop(0) if carried else None
    dq, dk, dv = rest[:3]
    if finished:
        keep, send, grads, held, sems, total = rest[3:]
    else:
        total, grads, held, sems = rest[3:]
    slot = pl.program_id(0)
    heads, _, width = q_ext.shape

    def fetch(which, head):
        source = raised.at[first_head + head, pl.ds((from_slot + which) * width, width)]
        return pltpu.make_async_copy(source, held.at[which * heads + head], sems.at[which * heads + head])

    @pl.when(slot == 0)
    def _():
        for which in range(held.shape[0] // heads):
            for head in range(heads):
                fetch(which, head).start()

    in_second = meta[2:3, :] > 0.5
    cos = jnp.where(in_second, cos_a[...], cos_b[...])
    sin = jnp.where(in_second, sin_a[...], sin_b[...])
    for head in range(heads):
        fetch(slot, head).wait()
        keys = k_ext[head]
        q_parts = []
        k_total = v_total = None
        for at in range(0, width, chunk):
            piece = slice(at, at + chunk)
            queries, outs = q_ext[head, :, piece], do_ext[head, :, piece]
            prob = held[slot * heads + head, piece, :]
            inner = dot(outs, v_ext[head], TN)
            score_grad = (prob.astype(f32) * inner).astype(bf16)
            q_parts.append(dot(keys[0:HEAD_DIM, :], score_grad, NT))
            k_part = dot(queries[0:HEAD_DIM, :], score_grad)
            v_part = dot(outs[0:HEAD_DIM, :], prob)
            k_total = k_part if k_total is None else k_total + k_part
            v_total = v_part if v_total is None else v_total + v_part
        for part, (out, grad) in enumerate(((dq, jnp.concatenate(q_parts, axis=1)), (dk, k_total), (dv, v_total))):
            one, two = grad[0:HALF, :], grad[HALF:HEAD_DIM, :]
            if part < 2:
                one, two = one * SCALE, two * SCALE
                one, two = one * cos + two * sin, two * cos - one * sin
            out[head, 0:HALF, :] = one.astype(bf16)
            out[head, HALF:HEAD_DIM, :] = two.astype(bf16)
            base = (part * heads + head) * HEAD_DIM
            grads[base : base + HEAD_DIM, :] = out[head]
    share = dot(low[...], grads[...], NT)
    rows = share.shape[0]

    @pl.when(slot == 0)
    def _():
        total[0:rows, :] = before[0:rows, :] + share if carried else share

    @pl.when(slot > 0)
    def _():
        total[0:rows, :] += share

    if finished:

        @pl.when(slot == pl.num_programs(0) - 1)
        def _():
            total[rows:, :] = jnp.zeros((total.shape[0] - rows, total.shape[1]), f32)
            split_halves(total, keep, send)


def middle_kernel(
    meta, x0, attended, inverse, outward, pair_all, embedding, vectors,
    dx1, do_ext, keep_pair, send_pair, keep_rest, send_rest, dtable, loss,
    w_up, w_down, up_t, down_t, act, slope, dw_up, dw_down, dw_out, dvec, vec, wide, table, table_t, w_out, w_out_t,
    sems,
):
    step = pl.program_id(0)
    chunks = pair_all.shape[1]
    model, width = x0.shape
    hidden_units = w_up.shape[1]
    unit = hidden_units // chunks
    heads = do_ext.shape[0]
    vocab = embedding.shape[0]

    @pl.when(step == 0)
    def _():
        fetches = []
        for side, into in enumerate((w_up, w_down)):
            for part in range(chunks):
                fetch = pltpu.make_async_copy(
                    pair_all.at[side, part], into.at[:, pl.ds(part * unit, unit)], sems.at[2 + side * chunks + part]
                )
                fetch.start()
                fetches.append(fetch)
        vec[...] = columns_of(vectors, wide)
        wide[...] = jnp.zeros_like(wide)
        wide[0:vocab, :] = embedding[...]
        table[...] = wide[0:VPAD, :].astype(bf16)
        table_t[...] = wide[...].T.astype(bf16)
        w_out[...] = outward[...].astype(bf16)
        w_out_t[...] = w_out[...].T
        dw_up[...] = jnp.zeros_like(dw_up)
        dw_down[...] = jnp.zeros_like(dw_down)
        dw_out[...] = jnp.zeros_like(dw_out)
        dtable[...] = jnp.zeros_like(dtable)
        dvec[...] = jnp.zeros_like(dvec)
        loss[...] = jnp.zeros_like(loss)
        for fetch in fetches:
            fetch.wait()
        for part in range(chunks):
            span = slice(part * unit, (part + 1) * unit)
            up_t[span, :] = w_up[:, span].T
            down_t[span, :] = w_down[:, span].T

    def col(index):
        return vec[:, index : index + 1]

    after = 8 + chunks_of_bias(model)
    x1 = x0[...] + dot(w_out_t[...], attended[...]) + col(5)
    hat_two, inverse_two = norm_stats(x1)
    c_low = (hat_two * col(6) + col(7)).astype(bf16)
    for first in range(0, hidden_units, UNITS):
        inner = dot(up_t[first : first + UNITS, :], c_low)
        for at in range(first, first + UNITS, model):
            hidden = inner[at - first : at - first + model, :] + col(8 + at // model)
            cdf = 0.5 + 0.5 * lax.erf(hidden * (0.5**0.5))
            density = jnp.exp(hidden * hidden * -0.5) * (1.0 / math.sqrt(2.0 * math.pi))
            act[at : at + model, :] = (hidden * cdf).astype(bf16)
            slope[at : at + model, :] = (cdf + hidden * density).astype(bf16)
    x2 = x1 + dot(w_down[...], act[...]) + col(after)
    hat_end, inverse_end = norm_stats(x2)
    f_low = (hat_end * col(after + 1) + col(after + 2)).astype(bf16)
    vocab_rows = rows_of(VPAD, width)
    logits = jnp.where(vocab_rows < vocab, dot(table[...], f_low), -MASKED)
    top = jnp.max(logits, axis=0, keepdims=True)
    raised = jnp.exp(logits - top)
    total = jnp.sum(raised, axis=0, keepdims=True)
    target = (vocab_rows == meta[1:2, :].astype(jnp.int32)).astype(f32)
    chosen = jnp.sum(logits * target, axis=0, keepdims=True)
    weight = meta[3:4, :]
    loss[0:1, :] += jnp.broadcast_to(lane_sum(weight * (jnp.log(total) + top - chosen)), (1, loss.shape[1]))
    logit_grad = (weight * (raised / total - target)).astype(bf16)
    dtable[...] += dot(logit_grad, f_low, NT)
    f_grad = dot(table_t[:, 0:VPAD], logit_grad)
    dvec[:, 4 + chunks : 5 + chunks] += lane_sum(f_grad * hat_end)
    dvec[:, 5 + chunks : 6 + chunks] += lane_sum(f_grad)
    x2_grad = norm_back(f_grad, hat_end, inverse_end, col(after + 1))
    g_low = x2_grad.astype(bf16)
    dvec[:, 3 + chunks : 4 + chunks] += lane_sum(g_low.astype(f32))
    dw_down[...] += dot(g_low, act[...], NT)
    for first in range(0, hidden_units, UNITS):
        span = slice(first, first + UNITS)
        act[span, :] = (dot(down_t[span, :], g_low) * slope[span, :]).astype(bf16)
    c_grad = dot(w_up[...], act[...])
    dw_up[...] += dot(c_low, act[...], NT)
    for part in range(hidden_units // model):
        dvec[:, 3 + part : 4 + part] += lane_sum(act[part * model : (part + 1) * model, :].astype(f32))

    @pl.when(step == pl.num_programs(0) - 1)
    def _():
        is_first = lax.axis_index("core") == 0
        for side, (low, here, there, out) in enumerate(
            ((down_t, dw_down, dw_up, send_pair), (up_t, dw_up, dw_down, keep_pair))
        ):
            for part in range(chunks):
                span = slice(part * unit, (part + 1) * unit)
                low[part * model : (part + 1) * model, :] = jnp.where(is_first, here[:, span], there[:, span]).astype(bf16)
            pltpu.make_async_copy(low, out, sems.at[side]).start()

    dvec[:, 1:2] += lane_sum(c_grad * hat_two)
    dvec[:, 2:3] += lane_sum(c_grad)
    x1_grad = x2_grad + norm_back(c_grad, hat_two, inverse_two, col(6))
    dx1[...] = x1_grad
    x1_low = x1_grad.astype(bf16)
    dvec[:, 0:1] += lane_sum(x1_low.astype(f32))
    dw_out[0:model, :] += dot(attended[...], x1_low, NT)
    o_grad = dot(w_out[...], x1_low)
    inner = o_grad * attended[...].astype(f32)
    row = rows_of(EXT - HEAD_DIM, width)
    for head in range(heads):
        span = slice(head * HEAD_DIM, (head + 1) * HEAD_DIM)
        share = inverse[head, 0:1, :]
        high, middle, rest = split3(-jnp.sum(inner[span, :], axis=0, keepdims=True) * share)
        do_ext[head, 0:HEAD_DIM, :] = (o_grad[span, :] * share).astype(bf16)
        tail = jnp.where(row == 0, high, jnp.where(row == 1, middle, jnp.where(row == 2, rest, 0.0)))
        do_ext[head, HEAD_DIM:EXT, :] = tail.astype(bf16)

    @pl.when(step == pl.num_programs(0) - 1)
    def _():
        dw_out[model:, :] = dvec[...].T
        split_halves(dw_out, keep_rest, send_rest)
        for side, (low, out) in enumerate(((down_t, send_pair), (up_t, keep_pair))):
            pltpu.make_async_copy(low, out, sems.at[side]).wait()


def chunks_of_bias(model):
    return FF // model


def input_back_kernel(meta, x0, dq, dk, dv, dx1, weight, vectors, dtable_in, *rest, last):
    if last:
        loss, dvec_in, tail, vec, wide, dvec, dtable = rest
    else:
        dvec, dtable, vec, wide = rest
    step = pl.program_id(0)
    model, width = x0.shape

    @pl.when(step == 0)
    def _():
        vec[...] = columns_of(vectors, wide)
        dtable[...] = dtable_in[...]
        dvec[...] = dvec_in[...] if last else jnp.zeros_like(dvec)

    back = None
    for part, grad in enumerate((dq, dk, dv)):
        share = dot(weight[:, part * model : (part + 1) * model], grad[...])
        back = share if back is None else back + share
    hat, inverse = norm_stats(x0[...])
    dvec[:, 0:1] += lane_sum(back * hat)
    dvec[:, 1:2] += lane_sum(back)
    dvec[0:1, 2:3] += lane_sum(meta[4:5, :])
    x0_grad = dx1[...] + norm_back(back, hat, inverse, vec[:, 0:1])
    onehot = (rows_of(VPAD, width) == meta[0:1, :].astype(jnp.int32)).astype(f32).astype(bf16)
    high = x0_grad.astype(bf16)
    for piece in (high, (x0_grad - high.astype(f32)).astype(bf16)):
        dtable[...] += dot(onehot, piece, NT)

    if last:

        @pl.when(step == pl.num_programs(0) - 1)
        def _():
            columns = dvec[...].T[0:8, :]
            tail[0:VOCAB_ROWS, 0:model] = dtable[0:VOCAB_ROWS, :]
            tail[VOCAB_ROWS:, 0:model] = jnp.where(rows_of(8, model) < 2, columns, 0.0)
            lane = lax.broadcasted_iota(jnp.int32, (TAIL, 128), 1)
            numbers = jnp.where(lane == 0, loss[0:1, 0:1], jnp.where(lane == 1, columns[2:3, 0:1], 0.0))
            tail[:, model:] = jnp.where(rows_of(TAIL, 128) == 0, numbers, 0.0)


def encode(tail):
    wide = tail.shape[1] - 128
    row = rows_of(tail.shape[0], 128)
    high, middle, rest = split3(tail[0:1, wide:])
    scalars = jnp.where(row == 0, high, jnp.where(row == 1, middle, jnp.where(row == 2, rest, 0.0)))
    return jnp.concatenate([tail[:, :wide], scalars], axis=1)


def decode(tail):
    wide = tail.shape[1] - 128
    row = rows_of(tail.shape[0], 128)
    total = tail[0:1, wide:] + tail[1:2, wide:] + tail[2:3, wide:]
    return jnp.concatenate([tail[:, :wide], jnp.where(row == 0, total, 0.0)], axis=1)


def pack_kernel(swapped, pair, tail, out, keep, send, *, pieces):
    shares = swapped[...].astype(f32)
    rows = shares.shape[0] // pieces
    total = None
    for at in range(pieces):
        share = shares[at * rows : (at + 1) * rows, :]
        total = share if total is None else total + share
    both = pair[...].astype(f32)
    half = keep.shape[0]
    first, second = both[0:half, :], both[half:, :]
    square = jnp.sum(lane_sum(first * first + second * second), axis=0, keepdims=True)
    is_first = lax.axis_index("core") == 0
    keep[...] = jnp.where(is_first, first, second).astype(bf16)
    send[...] = jnp.where(is_first, second, first).astype(bf16)
    values = tail[...]
    wide = values.shape[1] - 128
    at_square = (rows_of(values.shape[0], 128) == 0) & (lax.broadcasted_iota(jnp.int32, (values.shape[0], 128), 1) == 2)
    values = jnp.concatenate([values[:, :wide], values[:, wide:] + jnp.where(at_square, square, 0.0)], axis=1)
    out[...] = jnp.concatenate([total, encode(values)], axis=0).astype(bf16)


def stage_kernel(own, one, two, three, out, *, axis):
    index = lax.axis_index(axis)
    odd, high = lax.rem(index, 2) == 1, index >= 2
    values = [ref[...].astype(f32) for ref in (own, one, two, three)]
    rows = values[0].shape[0] - TAIL
    parts = [value[0:rows, :] for value in values]
    near = jnp.where(odd, parts[1], parts[0]), jnp.where(odd, parts[0], parts[1])
    far = jnp.where(odd, parts[3], parts[2]), jnp.where(odd, parts[2], parts[3])
    placed = [jnp.where(high, far[i], near[i]) for i in range(2)] + [jnp.where(high, near[i], far[i]) for i in range(2)]
    tails = [decode(value[rows:, :]) for value in values]
    total = (tails[0] + tails[1]) + (tails[2] + tails[3])
    out[...] = jnp.concatenate([*placed, encode(total)], axis=0).astype(bf16)


def adam_step(weight, grad, drift, spread, rate):
    drift = FIRST_DECAY * drift + (1.0 - FIRST_DECAY) * grad
    spread = SECOND_DECAY * spread + (1.0 - SECOND_DECAY) * grad * grad
    adjusted = (
        drift
        / (1.0 - FIRST_DECAY**STEP)
        / (jnp.sqrt(spread / (1.0 - SECOND_DECAY**STEP)) + ADAM_EPS)
    )
    return (weight - rate * (adjusted + WEIGHT_DECAY * weight), drift, spread)


def update_kernel(*refs, groups, early_groups):
    early_mine, early_other, last_mine, last_other, pair_keep, pair_sent = refs[:6]
    ins, outs = refs[6:21], refs[21:41]
    pair_out, norm_out, g_in, g_out, g_table, g_vec, scale, sems = refs[41:49]
    held = refs[49:]
    step = pl.program_id(0)
    steps = g_in.shape[0] // outs[4].shape[0]

    def copy(array, chunk):
        span = pl.ds(chunk * outs[4].shape[0], outs[4].shape[0])
        return pltpu.make_async_copy(ins[3 + array].at[span], held[array].at[span], sems.at[array, chunk])

    @pl.when(step == 0)
    def _():
        for chunk in range(steps):
            for array in range(6):
                copy(array, chunk).start()

    vocab, model = ins[0].shape
    half_rows = early_mine.shape[0]
    piece = model // groups
    after = model - half_rows

    @pl.when(step == 0)
    def _():
        is_first = lax.axis_index("core") == 0

        def halves(mine, other):
            mine, other = mine[0:half_rows, :].astype(f32), other[0:half_rows, :].astype(f32)
            return jnp.where(is_first, mine, other), jnp.where(is_first, other, mine)

        squares = jnp.zeros((1, 128), f32)

        def add_squares(values):
            rows = jnp.sum(values * values, axis=0, keepdims=True)
            total = None
            for at in range(0, rows.shape[1], 128):
                total = rows[:, at : at + 128] if total is None else total + rows[:, at : at + 128]
            return total

        for mine, other, first, size in (
            (early_mine, early_other, 0, early_groups),
            (last_mine, last_other, early_groups, groups - early_groups),
        ):
            upper, lower = halves(mine, other)
            if first == 0:
                rest_upper, rest_lower = upper[:, 3 * piece * size :], lower[:, 3 * piece * size :]
            upper, lower = upper[:, : 3 * piece * size], lower[:, : 3 * piece * size]
            squares += add_squares(upper) + add_squares(lower)
            for group in range(size):
                for part in range(3):
                    source = slice((group * 3 + part) * piece, (group * 3 + part + 1) * piece)
                    at = part * model + (first + group) * piece
                    g_in[0:half_rows, at : at + piece] = upper[:, source]
                    g_in[half_rows:model, at : at + piece] = lower[0:after, source]
                    into = slice((first + group) * piece, (first + group + 1) * piece)
                    g_vec[2 + part : 3 + part, into] = lower[after : after + 1, source]
        upper, lower = rest_upper, rest_lower
        g_out[0:half_rows, :] = upper
        g_out[half_rows:, :] = lower[0:after, :]
        others = lower[after : after + 16, :]
        g_vec[5:15, :] = others[0:10, :]
        tails = [decode(ref[half_rows:, :].astype(f32)) for ref in (last_mine, last_other)]
        final = tails[0] + tails[1]
        scalars = final[:, model:]
        table = final[0:VOCAB_ROWS, 0:model]
        g_table[...] = table
        tail = final[VOCAB_ROWS:, 0:model]
        g_vec[0:2, :] = tail[0:2, :]
        squares += add_squares(upper) + add_squares(lower[0:after, :]) + add_squares(others) + add_squares(table)
        squares += add_squares(tail[0:2, :])
        total = lane_sum(squares) + scalars[0:1, 2:3]
        crops = scalars[0:1, 1:2]
        norm = jnp.sqrt(total) / crops
        scale[...] = jnp.broadcast_to(jnp.minimum(1.0, CLIP_NORM / (norm + 1e-06)) / crops, scale.shape)
        pair_out[0] = jnp.sum(scalars[0:1, 0:1])
        pair_out[1] = jnp.sum(crops)
        norm_out[0] = jnp.sum(norm)

    factor = scale[0:1, 0:1]

    def update(which, grad, rate, span=...):
        source = held[which * 3 - 3 : which * 3] if span is not ... else ins[which * 3 : which * 3 + 3]
        weight, drift, spread = (ref[span] for ref in source)
        fresh, drift, spread = adam_step(weight, grad * factor, drift, spread, rate)
        out = outs[which * 4 : which * 4 + 4]
        out[0][...] = fresh
        out[1][...] = drift
        out[2][...] = spread
        out[3][...] = fresh.astype(bf16)

    @pl.when(step == 0)
    def _():
        update(0, g_table[0:vocab, :], 0.05)
        keep, sent = pair_keep[...].astype(f32), pair_sent[...].astype(f32)
        is_first = lax.axis_index("core") == 0
        update(3, jnp.stack([jnp.where(is_first, keep, sent), jnp.where(is_first, sent, keep)]), 0.05)
        update(4, g_vec[0:15, :], 0.2)

    for array in range(6):
        copy(array, step).wait()
    rows = outs[4].shape[0]
    span = pl.ds(pl.multiple_of(step * rows, rows), rows)
    update(1, g_in[span, :], 0.05, span)
    update(2, g_out[span, :], 0.1, span)


def whole(shape):
    return pl.BlockSpec(shape, lambda *_: (0,) * len(shape), pipeline_mode=pl.Buffered(1))


def shaped(shape, dtype):
    return jax.ShapeDtypeStruct(shape, dtype)


def limits(mib):
    return pltpu.CompilerParams(vmem_limit_bytes=mib * MIB)


def cost(flops, moved, transcendentals=0):
    return pl.CostEstimate(flops=int(flops), bytes_accessed=int(moved), transcendentals=int(transcendentals))


def rotary_constants(rows):
    freq = np.float32(10000.0) ** (-np.arange(0, HEAD_DIM, 2, dtype=np.float32) / np.float32(HEAD_DIM))
    angle = np.arange(rows, dtype=np.float32)[None, :] * freq[:, None].astype(np.float32)
    return np.cos(angle).astype(np.float32), np.sin(angle).astype(np.float32)


def body(
    columns,
    deep,
    true_ids,
    picked,
    replace_kinds,
    random_ids,
    splits,
    embedding,
    projection,
    outward,
    feedforward,
    vectors,
    embedding_drift,
    embedding_spread,
    projection_drift,
    projection_spread,
    outward_drift,
    outward_spread,
    feedforward_drift,
    feedforward_spread,
    vectors_drift,
    vectors_spread,
):
    tokens = true_ids.shape[0]
    slots = splits.shape[0]
    rows = tokens // slots
    half = rows // 2
    vocab, model = embedding.shape
    heads = model // HEAD_DIM
    bias_rows = chunks_of_bias(model)
    block = half
    blocks = tokens // block
    wide = FF // columns
    devices = columns * deep * 2
    chips = ("col", "deep")
    everywhere = ("col", "deep", "core")

    pair_all = lax.all_gather(feedforward.astype(bf16), everywhere, axis=1, tiled=True)
    pair_all = pair_all.reshape(2, columns, model, wide)

    cos_np, sin_np = rotary_constants(rows)
    cos_table, sin_table = jnp.asarray(cos_np), jnp.asarray(sin_np)
    twice_cos, twice_sin = (jnp.asarray(np.tile(t[:, :half], (1, 2))) for t in (cos_np, sin_np))

    def by_block(count):
        return pl.BlockSpec((count, block), lambda i: (0, i))

    def heads_block(count):
        return pl.BlockSpec((heads, count, block), lambda i: (0, 0, i))

    first_half = pl.BlockSpec((HALF, block), lambda i: (0, 0))
    own_half = pl.BlockSpec((HALF, block), lambda i: (0, i % 2))
    id_block = pl.BlockSpec((1, block), lambda i: (0, i))
    meta, x0, normed, q_ext, k_ext, v_ext, qkv_low = pl.pallas_call(
        qkv_kernel,
        grid=(blocks,),
        in_specs=[id_block] * 4 + [pl.BlockSpec((1, rows), lambda i: (0, i // 2)), pl.BlockSpec(memory_space=pltpu.SMEM),
                  whole((vocab, model)), whole((model, 3 * model)), whole(vectors.shape),
                  first_half, own_half, first_half, own_half],
        out_specs=[by_block(8), by_block(model), by_block(model + 16), heads_block(EXT), heads_block(EXT), heads_block(EXT),
                   whole((model, 3 * model))],
        out_shape=[shaped((8, tokens), f32), shaped((model, tokens), f32), shaped((model + 16, tokens), bf16)]
        + [shaped((heads, EXT, tokens), bf16)] * 3 + [shaped((model, 3 * model), bf16)],
        scratch_shapes=[pltpu.VMEM((model, 128), bf16), pltpu.VMEM((3 * model, model), bf16), pltpu.VMEM((model, 128), f32),
                        pltpu.VMEM((128, model), f32)],
        compiler_params=limits(56),
        cost_estimate=cost(2 * 3 * model * model * tokens, 20 * model * tokens),
        name="embed_and_qkv",
    )(*(ids.reshape(1, tokens) for ids in (true_ids, picked, replace_kinds, random_ids, picked)), splits,
      embedding, projection, vectors, cos_table, cos_table, sin_table, sin_table)

    per = 4

    def head_group(count, size, first=0):
        return pl.BlockSpec((size, count, rows), lambda s, g: (first + g, 0, s))

    attended, raised, inverse = pl.pallas_call(
        attention_kernel,
        grid=(slots, heads // per),
        in_specs=[head_group(EXT, per)] * 3,
        out_specs=[head_group(HEAD_DIM, per), pl.BlockSpec((per, rows, rows), lambda s, g: (g, s, 0)), head_group(8, per)],
        out_shape=[shaped((heads, HEAD_DIM, tokens), bf16), shaped((heads, tokens, rows), bf16), shaped((heads, 8, tokens), f32)],
        compiler_params=limits(56),
        cost_estimate=cost(2 * 16 * model * rows * tokens, 2 * heads * rows * tokens, heads * rows * tokens),
        name="attention",
    )(q_ext, k_ext, v_ext)
    attended = attended.reshape(model, tokens)

    half_rows = (model + 128) // 2
    owned = -(-half_rows // (8 * columns * deep)) * 8
    dx1, do_ext, keep_pair, send_pair, keep_rest, send_rest, dtable_end, loss = pl.pallas_call(
        middle_kernel,
        grid=(blocks,),
        in_specs=[by_block(8), by_block(model), by_block(model), heads_block(8), whole((model, model)),
                  pl.BlockSpec(memory_space=pl.ANY), whole((vocab, model)), whole(vectors.shape)],
        out_specs=[by_block(model), heads_block(EXT), pl.BlockSpec(memory_space=pl.ANY), pl.BlockSpec(memory_space=pl.ANY),
                   whole((half_rows, model)), whole((half_rows, model)), whole((VPAD, model)), whole((8, 128))],
        out_shape=[shaped((model, tokens), f32), shaped((heads, EXT, tokens), bf16), shaped((columns * model, wide), bf16),
                   shaped((columns * model, wide), bf16), shaped((half_rows, model), bf16), shaped((half_rows, model), bf16),
                   shaped((VPAD, model), f32), shaped((8, 128), f32)],
        scratch_shapes=[pltpu.VMEM((model, FF), bf16), pltpu.VMEM((model, FF), bf16), pltpu.VMEM((FF, model), bf16),
                        pltpu.VMEM((FF, model), bf16), pltpu.VMEM((FF, block), bf16), pltpu.VMEM((FF, block), bf16),
                        pltpu.VMEM((model, FF), f32), pltpu.VMEM((model, FF), f32),
                        pltpu.VMEM((model + 128, model), f32), pltpu.VMEM((model, 128), f32),
                        pltpu.VMEM((model, 128), f32), pltpu.VMEM((128, model), f32),
                        pltpu.VMEM((VPAD, model), bf16), pltpu.VMEM((model, 128), bf16),
                        pltpu.VMEM((model, model), bf16), pltpu.VMEM((model, model), bf16), pltpu.SemaphoreType.DMA((2 + 2 * columns,))],
        compiler_params=limits(62),
        cost_estimate=cost(2 * tokens * model * (6 * FF + 3 * model), 14 * model * tokens + 16 * model * FF, FF * tokens),
        name="feedforward_and_head",
    )(meta, x0, attended, inverse, outward, pair_all, embedding, vectors)

    count = columns * deep

    def swap(values, axes):
        return lax.all_to_all(values, axes, 0, 0, tiled=True)

    def over_core(values):
        return lax.ppermute(values, "core", [(0, 1), (1, 0)])

    def add_up(values, pieces):
        return jnp.sum(values.reshape((pieces, -1) + values.shape[1:]).astype(f32), axis=0)

    def pair_sum(keep, sent):
        return (keep.astype(f32) + sent.astype(f32)).astype(bf16)

    def pad_rows(values):
        return jnp.pad(values, ((0, owned * count - half_rows), (0, 0)))

    def to_owner(values):
        return swap(pad_rows(values), chips)

    def gather4(values, axis):
        one, two, three = (lax.ppermute(values, axis, [(i, i ^ d) for i in range(4)]) for d in (1, 2, 3))
        index = lax.axis_index(axis)
        odd, high = index % 2 == 1, index >= 2
        near = jnp.where(odd, one, values), jnp.where(odd, values, one)
        far = jnp.where(odd, three, two), jnp.where(odd, two, three)
        return jnp.concatenate(
            [jnp.where(high, far[i], near[i]) for i in range(2)] + [jnp.where(high, near[i], far[i]) for i in range(2)],
            axis=0,
        )

    def gather_deep(values):
        return gather4(values, "deep") if deep == 4 else lax.all_gather(values, "deep", axis=0, tiled=True)

    def gather_col(values):
        return (gather4(values, "col") if columns == 4 else lax.all_gather(values, "col", axis=0, tiled=True))[:half_rows]

    def together(first, *others):
        return lax.optimization_barrier((first, *others))

    pair_sent, rest_sent = over_core(send_pair), over_core(send_rest)
    per_call = 4
    width = 3 * per_call * HEAD_DIM
    grads = None
    keeps, sents = [], []
    groups = heads // per_call
    calls = [(g, 0, slots) for g in range(groups)]
    carry = None
    for index, (first, from_slot, slot_count) in enumerate(calls):
        chained, carried, finished = grads is not None, carry is not None, from_slot + slot_count == slots

        def group(count, first=first, from_slot=from_slot):
            return pl.BlockSpec((per_call, count, rows), lambda s: (first, 0, from_slot + s))

        def by_slot(count, from_slot=from_slot):
            return pl.BlockSpec((count, rows), lambda s: (0, from_slot + s))

        table_spec = pl.BlockSpec((HALF, rows), lambda s: (0, 0))
        outs = pl.pallas_call(
            functools.partial(attention_back_kernel, chunk=half, chained=chained, carried=carried, finished=finished,
                              first_head=first * per_call, from_slot=from_slot),
            grid=(slot_count,),
            in_specs=[group(EXT)] * 4 + [pl.BlockSpec(memory_space=pl.ANY), by_slot(model + 16), by_slot(8)] + [table_spec] * 4
            + [pl.BlockSpec(memory_space=pl.ANY)] * (3 if chained else 0)
            + ([whole((2 * half_rows, width))] if carried else []),
            out_specs=[group(HEAD_DIM)] * 3
            + ([pl.BlockSpec((half_rows, width), lambda s: (0, 0))] * 2 if finished else [whole((2 * half_rows, width))]),
            out_shape=[shaped((heads, HEAD_DIM, tokens), bf16)] * 3
            + ([shaped((half_rows, width), bf16)] * 2 if finished else [shaped((2 * half_rows, width), f32)]),
            scratch_shapes=[pltpu.VMEM((width, rows), bf16), pltpu.VMEM((slot_count * per_call, rows, rows), bf16),
                            pltpu.SemaphoreType.DMA((slot_count * per_call,))]
            + ([pltpu.VMEM((2 * half_rows, width), f32)] if finished else []),
            input_output_aliases={11: 0, 12: 1, 13: 2} if chained else {},
            compiler_params=limits(56),
            cost_estimate=cost(2 * 40 * width // 3 * rows * rows * slot_count, 20 * width * rows * slot_count, per_call * rows * rows * slot_count),
            name="attention_back",
        )(q_ext, k_ext, v_ext, do_ext, raised, normed, meta, twice_cos, cos_table, twice_sin, sin_table, *(grads or ()),
          *((carry,) if carried else ()))
        grads = list(outs[:3])
        carry = None if finished else outs[3]
        if finished:
            keeps.append(outs[3])
            sents.append(over_core(outs[4]))
        if index == 0:
            grads[0], pair_sent, rest_sent = together(grads[0], pair_sent, rest_sent)
            pair = pair_sum(keep_pair.reshape(count, -1, wide), pair_sent.reshape(count, -1, wide))
            rest_half = pad_rows(pair_sum(keep_rest, rest_sent)).reshape(count, owned, model)
            pair = jnp.concatenate([pair, rest_half], axis=1).reshape(-1, wide)
            do_ext, pair = together(do_ext, pair)
            pair = lax.psum_scatter(pair, "col", scatter_dimension=0, tiled=True)
        elif first == groups - 3:
            do_ext, pair = together(do_ext, pair)
            pair = lax.psum_scatter(pair, "deep", scatter_dimension=0, tiled=True)
        elif first == groups - 2:
            early = jnp.concatenate([pair_sum(keeps[i], sents[i]) for i in range(groups - 2)], axis=1)
            do_ext, early = together(do_ext, early)
            early = to_owner(early)
        elif first == groups - 1:
            late_half = jnp.concatenate([pair_sum(keeps[i], sents[i]) for i in range(groups - 2, groups)], axis=1)
            early = add_up(early, count).astype(bf16)
            dx1, late_half, early, pair = together(dx1, late_half, early, pair)
            late_half = to_owner(late_half)
            early = gather_deep(jnp.concatenate([early, pair[-owned:]], axis=1))
            pair = pair[:-owned]
    dq, dk, dv = (grad.reshape(model, tokens) for grad in grads)

    back_out = [shaped((model, 128), f32), shaped((VPAD, model), f32)]
    back_room = [pltpu.VMEM((model, 128), f32), pltpu.VMEM((128, model), f32)]

    def input_back(part, extra):
        def by_part(rows_):
            return pl.BlockSpec((rows_, block), lambda i: (0, i + part * (blocks // 2)))

        last = part == 1
        room = [pltpu.VMEM(shape.shape, f32) for shape in back_out]
        return pl.pallas_call(
            functools.partial(input_back_kernel, last=last),
            grid=(blocks // 2,),
            in_specs=[by_part(8)] + [by_part(model)] * 5 + [whole((model, 3 * model)), whole(vectors.shape)]
            + [whole(array.shape) for array in extra],
            out_specs=[whole((TAIL, model + 128))] if last else [whole(shape.shape) for shape in back_out],
            out_shape=[shaped((TAIL, model + 128), f32)] if last else back_out,
            scratch_shapes=back_room + (room if last else []),
            compiler_params=limits(56),
            cost_estimate=cost(model * model * tokens, 4 * model * tokens),
            name="input_back",
        )(meta, x0, dq, dk, dv, dx1, qkv_low, vectors, *extra)

    halfway = input_back(0, (dtable_end,))
    dvec_half, dtable_half, early = together(*halfway, early)
    early = gather_col(early)
    (tail,) = input_back(1, (dtable_half, loss, dvec_half))
    tail, pair, early, late_half = together(tail, pair, early, late_half)
    early_other = over_core(early)

    def call_small(kernel, args, outs, name):
        return pl.pallas_call(
            kernel,
            in_specs=[pl.BlockSpec(memory_space=pltpu.VMEM)] * len(args),
            out_specs=[pl.BlockSpec(memory_space=pltpu.VMEM)] * len(outs),
            out_shape=[shaped(shape, bf16) for shape in outs],
            compiler_params=limits(40),
            cost_estimate=cost(1e6, 4e6),
            name=name,
        )(*args)

    own = pair.shape[0] // 2
    last_width = late_half.shape[1]
    if columns == 4 and deep == 4 and last_width == tail.shape[1]:
        packed, pair_keep, pair_sent = call_small(
            functools.partial(pack_kernel, pieces=count), (late_half, pair, tail),
            [(owned + TAIL, last_width), (own, wide), (own, wide)], "pack",
        )
        pair_sent = over_core(pair_sent)
        for axis in ("deep", "col"):
            got = [lax.ppermute(packed, axis, [(i, i ^ d) for i in range(4)]) for d in (1, 2, 3)]
            merged = 4 * (packed.shape[0] - TAIL) + TAIL
            (packed,) = call_small(functools.partial(stage_kernel, axis=axis), (packed, *got), [(merged, last_width)], "stage")
    else:
        is_first = lax.axis_index("core") == 0
        pair_keep = jnp.where(is_first, pair[:own], pair[own:])
        pair_sent = over_core(jnp.where(is_first, pair[own:], pair[:own]))
        square = jnp.sum(jnp.square(pair.astype(f32)))
        tail = lax.psum(tail.at[0, model + 2].add(square), chips)
        scalars = tail[0:1, model:]
        high = lax.reduce_precision(scalars, 8, 7)
        middle = lax.reduce_precision(scalars - high, 8, 7)
        numbers = jnp.concatenate([high, middle, scalars - high - middle, jnp.zeros((TAIL - 3, 128), f32)], axis=0)
        tail = jnp.pad(jnp.concatenate([tail[:, :model], numbers], axis=1), ((0, 0), (0, last_width - tail.shape[1])))
        packed = gather_col(gather_deep(add_up(late_half, count).astype(bf16)))
        packed = jnp.concatenate([packed, tail.astype(bf16)], axis=0)
    packed_other = over_core(packed)

    steps = 10
    state = (
        (embedding, embedding_drift, embedding_spread),
        (projection, projection_drift, projection_spread),
        (outward, outward_drift, outward_spread),
        (feedforward, feedforward_drift, feedforward_spread),
        (vectors, vectors_drift, vectors_spread),
    )

    def state_spec(array):
        if array.shape[0] == model:
            return pl.BlockSpec((model // steps, array.shape[1]), lambda i: (i, 0))
        return whole(array.shape)

    grads_in = (early, early_other, packed, packed_other, pair_keep, pair_sent)
    results = pl.pallas_call(
        functools.partial(update_kernel, groups=groups, early_groups=groups - 2),
        grid=(steps,),
        in_specs=[whole(array.shape) for array in grads_in] + [
            pl.BlockSpec(memory_space=pl.ANY) if array.shape[0] == model else whole(array.shape) for three in state for array in three
        ],
        out_specs=[state_spec(three[0]) for three in state for _ in range(4)]
        + [pl.BlockSpec(memory_space=pltpu.SMEM)] * 2,
        out_shape=[shaped(three[0].shape, dtype) for three in state for dtype in (f32, f32, f32, bf16)]
        + [shaped((2,), f32), shaped((1,), f32)],
        scratch_shapes=[pltpu.VMEM((model, 3 * model), f32), pltpu.VMEM((model, model), f32), pltpu.VMEM((VOCAB_ROWS, model), f32),
                        pltpu.VMEM((16, model), f32), pltpu.VMEM((8, 128), f32), pltpu.SemaphoreType.DMA((6, steps))]
        + [pltpu.VMEM(array.shape, f32) for three in state[1:3] for array in three],
        compiler_params=limits(56),
        cost_estimate=cost(60 * 4 * model * model, 4 * 30 * model * model),
        name="clip_and_adamw",
    )(*grads_in, *(array for three in state for array in three))
    return (results[20], results[21].reshape(()), *results[:20])


def solution(mesh):
    columns, row = mesh.shape["col"], mesh.shape["row"]
    fine = jax.sharding.Mesh(mesh.devices.reshape(columns, row // 2, 2), ("col", "deep", "core"))
    split_all, tiles, full = P(("col", "deep", "core")), P(None, ("deep", "core"), "col"), P()
    return jax.shard_map(
        functools.partial(body, columns, row // 2),
        mesh=fine,
        in_specs=(split_all,) * 5 + (full,) * 3 + (tiles,) + (full,) * 7 + (tiles,) * 2 + (full,) * 2,
        out_specs=(full,) * 14 + (tiles,) * 4 + (full,) * 4,
        check_vma=False,
    )
```
